32 devices in a mesh: ctx: 8 (over z, x), tp: 4 (over y, core).
Axes of the slice: x: 2, y: 2, z: 4, core: 2. Of those that a mesh axis runs over, the one named last changes fastest.
Arguments:
- query_key_value_input: bfloat16 [3, 8192, 2048], P(None, 'tp', 'ctx'), may hold values from -6 to 6
- featurizer_weights: float32 [3, 7, 8192], P(None, None, 'tp'), may hold values from -2.4 to 2.4
- channel_skip_scale: float32 [8192], P(('tp', 'ctx')), may hold values from -4 to 4
- group_long_filters: float32 [512, 2048], P(('tp', 'ctx')), may hold values from -1 to 1, as said below
- frozen_weight: bfloat16 [4096, 8192], P('ctx', 'tp'), may hold values from -4 to 4
- down_update_weight: bfloat16 [16, 8192], P(None, 'tp'), may hold values from -0.0625 to 0.0625
- up_update_weight: bfloat16 [4096, 16], P('ctx'), may hold values from -1.5 to 1.5
- magnitude: float32 [4096], replicated, may hold values from 0.5 to 2
Outputs:
- projected: bfloat16 [4096, 2048], P('tp', 'ctx')
The draws below stay inside these ranges and needn't reach their ends.
Inputs may be any that keep to these rules, and one draw needn't show every extreme that they name: `group_long_filters`: row g is the filter of channels g * 16 to g * 16 + 16 - 1 over lags 0 to 2047.
All inputs are finite; a program needn't handle non-finite values.
Results may differ from the reference program's by a relative error of at most 0.007.
Values may be sent and summed in bfloat16 or wider, within the bound.
No kernel may reach another device: no remote copies, remote signals or barrier semaphores. Data moves between devices by JAX's collectives and lax.ppermute only.
A program may use at most 192 MiB of HBM per device.

```python
import math
import jax
import jax.numpy as jnp
from jax import lax

MODEL_WIDTH = 8192
OUTPUT_FEATURES = 4096
GROUP = 16
TAPS = 7
UPDATE_RANK = 16
SEQUENCE_TOKENS = 2048
FILTER_GROUPS = 512


def draw_group_long_filters(key, part):
    key = jax.random.fold_in(key, 11)
    random_subkeys = jax.random.split(key, 6)
    tap_noise = jax.random.truncated_normal(random_subkeys[0], -3.8, 3.8, (FILTER_GROUPS, SEQUENCE_TOKENS), jnp.float32)
    slow_share = 0.5
    slow_group = jax.random.uniform(random_subkeys[1], (FILTER_GROUPS,), jnp.float32) < slow_share
    fast_span = 30.0 + 20.0 * jax.random.uniform(random_subkeys[2], (FILTER_GROUPS,), jnp.float32)
    slow_span = SEQUENCE_TOKENS * (2.0 + 4.0 * jax.random.uniform(random_subkeys[3], (FILTER_GROUPS,), jnp.float32))
    decay_span = jnp.where(slow_group, slow_span, fast_span)
    tail_level = jnp.where(slow_group, 0.0, jnp.sqrt(0.2 * fast_span / SEQUENCE_TOKENS))
    token_positions = jnp.arange(SEQUENCE_TOKENS, dtype=jnp.float32)
    decay_envelope = jnp.exp(-token_positions[None, :] / decay_span[:, None])
    decay_envelope = decay_envelope + tail_level[:, None] * jnp.exp(-token_positions[None, :] / slow_span[:, None])
    spike_position = jax.random.randint(random_subkeys[4], (FILTER_GROUPS, 3), 1, SEQUENCE_TOKENS)
    spike_falloff = jax.random.uniform(random_subkeys[5], (FILTER_GROUPS, 3), jnp.float32, 0.55, 0.8)
    for spike_index in range(3):
        reached_mask = token_positions[None, :] >= spike_position[:, spike_index:spike_index + 1].astype(jnp.float32)
        decay_envelope = decay_envelope * jnp.where(reached_mask, spike_falloff[:, spike_index:spike_index + 1], 1.0)
    norming = jnp.sqrt(2.0 / jnp.minimum(decay_span, SEQUENCE_TOKENS * 1.0)) / (1.0 + tail_level)
    return (tap_noise * decay_envelope * norming[:, None]).astype(jnp.float32)


def draw_frozen_weight(key, part):
    key = jax.random.fold_in(key, 23)
    random_subkeys = jax.random.split(key, 3)
    inputs_index = jnp.arange(MODEL_WIDTH, dtype=jnp.float32)
    input_scale = jnp.power(10.0, 0.5 * inputs_index / MODEL_WIDTH + 0.5 * jax.random.uniform(random_subkeys[0], (MODEL_WIDTH,), jnp.float32))
    output_scale = jnp.power(10.0, jax.random.uniform(random_subkeys[1], (OUTPUT_FEATURES,), jnp.float32))
    entries = jax.random.truncated_normal(random_subkeys[2], -4.0, 4.0, (OUTPUT_FEATURES, MODEL_WIDTH), jnp.float32)
    weights = entries * output_scale[:, None] * input_scale[None, :] * (0.2 / math.sqrt(MODEL_WIDTH))
    return weights.astype(jnp.bfloat16)


def block_scale(rng, extent, cuts, smallest, largest):
    def one(position, parts):
        steps = jax.random.uniform(jax.random.fold_in(jax.random.fold_in(rng, 6), position), (parts,), jnp.float32, smallest / len(cuts), largest / len(cuts))
        return jnp.repeat(jnp.exp(steps), extent[position] // parts).reshape((-1,) + (1,) * (len(extent) - position - 1))

    factor_of = one(*cuts[0])
    for cut in cuts[1:]:
        factor_of = factor_of * one(*cut)
    return factor_of


def noise(key, dims, width, limit, cuts=(), kind=jnp.bfloat16):
    level = block_scale(key, dims, cuts, -0.22, 0.18) if cuts else 1.0
    values = jax.random.normal(key, dims, jnp.float32) * width * level
    return jnp.minimum(jnp.maximum(values, -limit), limit).astype(kind)


def setup_inputs(seed: int = 0) -> dict:
    key_of = jax.random.split(jax.random.key(seed), 9)
    query_key_value_input = noise(key_of[0], (3, MODEL_WIDTH, SEQUENCE_TOKENS), 1.0, 6.0, ((1, 4), (2, 8)))
    featurizer_weights = noise(key_of[1], (3, TAPS, MODEL_WIDTH), 0.4, 2.4, ((2, 4),), jnp.float32)
    channel_skip_scale = noise(key_of[2], (MODEL_WIDTH,), 1.0, 4.0, ((0, 32),), jnp.float32)
    group_long_filters = draw_group_long_filters(jax.random.fold_in(key_of[8], 71), 0)
    frozen_weight = draw_frozen_weight(jax.random.fold_in(key_of[8], 71), 0)
    down_update_weight = noise(key_of[5], (UPDATE_RANK, MODEL_WIDTH), MODEL_WIDTH ** -0.5, 0.0625, ((1, 4),))
    up_update_weight = noise(key_of[6], (OUTPUT_FEATURES, UPDATE_RANK), 0.25, 1.5, ((0, 8),))
    magnitude = jnp.clip(jnp.exp(jax.random.uniform(key_of[7], (OUTPUT_FEATURES,), jnp.float32, math.log(0.5), math.log(2.0))), 0.5, 2.0)
    return {"query_key_value_input": query_key_value_input, "featurizer_weights": featurizer_weights, "channel_skip_scale": channel_skip_scale, "group_long_filters": group_long_filters, "frozen_weight": frozen_weight, "down_update_weight": down_update_weight, "up_update_weight": up_update_weight, "magnitude": magnitude}


EPSILON = 1e-06

def featurize(inputs_block, taps_block):
    values = inputs_block.astype(jnp.float32)
    length = inputs_block.shape[-1]
    padded = jnp.pad(values, ((0, 0), (0, 0), (TAPS - 1, 0)))
    result = jnp.zeros(values.shape, jnp.float32)
    for offset in range(TAPS):
        starting = TAPS - 1 - offset
        result = result + taps_block[:, offset, :, None] * padded[:, :, starting:starting + length]
    return result

def channel_block(pieces):
    inputs_block, taps_block, skip_block, filters = pieces
    featured = featurize(inputs_block, taps_block)
    mixture = (featured[1] * featured[2]).astype(jnp.bfloat16)
    mixture_wide = lax.optimization_barrier(mixture).astype(jnp.float32)
    length = inputs_block.shape[-1]
    spectrum = jnp.fft.rfft(mixture_wide, n=2 * length, axis=-1)
    response = jnp.repeat(jnp.fft.rfft(filters, n=2 * length, axis=-1), GROUP, axis=0)
    convolved = jnp.fft.irfft(spectrum * response, n=2 * length, axis=-1)[:, :length]
    summed = (convolved + skip_block[:, None] * mixture_wide).astype(jnp.bfloat16)
    summed_wide = lax.optimization_barrier(summed).astype(jnp.float32)
    return (featured[0] * summed_wide).astype(jnp.bfloat16)

def reference(query_key_value_input, featurizer_weights, channel_skip_scale, group_long_filters, frozen_weight, down_update_weight, up_update_weight, magnitude):
    block_count = 16
    block_width = MODEL_WIDTH // block_count
    inputs_blocks = query_key_value_input.reshape(3, block_count, block_width, SEQUENCE_TOKENS).transpose(1, 0, 2, 3)
    taps_blocks = featurizer_weights.reshape(3, TAPS, block_count, block_width).transpose(2, 0, 1, 3)
    skip_blocks = channel_skip_scale.reshape(block_count, block_width)
    filter_blocks = group_long_filters.reshape(block_count, block_width // GROUP, SEQUENCE_TOKENS)
    gating = lax.map(channel_block, (inputs_blocks, taps_blocks, skip_blocks, filter_blocks)).reshape(MODEL_WIDTH, SEQUENCE_TOKENS)
    lowrank_update = jnp.dot(up_update_weight, down_update_weight, preferred_element_type=jnp.float32)
    merged = (frozen_weight.astype(jnp.float32) + lowrank_update).astype(jnp.bfloat16)
    merged_wide = lax.optimization_barrier(merged).astype(jnp.float32)
    row_norm = lax.optimization_barrier(jnp.sum(merged_wide * merged_wide, axis=1))
    partial_value = jnp.dot(merged, gating, preferred_element_type=jnp.float32)
    scaling = magnitude / jnp.sqrt(row_norm + EPSILON)
    return (partial_value * scaling[:, None]).astype(jnp.bfloat16)
```

```python
import functools

import jax
import jax.numpy as jnp
from jax import lax
from jax.experimental import pallas as pl
from jax.experimental.pallas import tpu as pltpu
from jax.sharding import PartitionSpec as P

GROUP = 16
TAPS = 7
EPSILON = 1e-06
MIB = 1 << 20
BF16 = jnp.bfloat16
F32 = jnp.float32


def exchange(block, axis, distance):
    count = lax.axis_size(axis)
    return lax.ppermute(block, axis, [(i, i ^ distance) for i in range(count)])


def whole_spec(shape):
    return pl.BlockSpec(shape, lambda *_: (0,) * len(shape))


def featurize_kernel(first, count, where_ref, input_ref, taps_ref, halo_ref, *refs):
    out_refs, (taps_turned, halo_turned) = refs[:-2], refs[-2:]
    step = pl.program_id(0)
    block, tokens = input_ref.shape[1:]
    lanes = taps_ref.shape[2]
    taps_turned[...] = jnp.concatenate(
        [taps_ref[i, j : j + 1, :] for i in range(3) for j in range(TAPS)]
        + [jnp.zeros((128 - 3 * TAPS, lanes), F32)],
        axis=0,
    ).T
    halo_rows = halo_ref[...].astype(F32)
    halo_turned[...] = jnp.concatenate(
        [halo_rows, jnp.zeros((128 - halo_rows.shape[0], lanes), F32)], axis=0
    ).T
    dest = jnp.bitwise_xor(step + first, where_ref[0])
    here = pl.ds(pl.multiple_of(lax.rem(dest * block, lanes), block), block)
    taps, halo = taps_turned[here, :], halo_turned[here, :]
    lane = lax.broadcasted_iota(jnp.int32, (block, 128), 1)
    features = []
    for i in range(3):
        values = input_ref[i].astype(F32)
        before = pltpu.roll(halo, (128 - (TAPS - 1) - (TAPS - 1) * i) % 128, 1)
        tiles = [before] + [values[:, s : s + 128] for s in range(0, tokens, 128)]
        sums = [tiles[n + 1] * taps[:, i * TAPS : i * TAPS + 1] for n in range(tokens // 128)]
        for j in range(1, TAPS):
            turned = [pltpu.roll(tile, j, 1) for tile in tiles]
            weight = taps[:, i * TAPS + j : i * TAPS + j + 1]
            for n in range(tokens // 128):
                sums[n] = sums[n] + weight * jnp.where(lane < j, turned[n], turned[n + 1])
        features.append(jnp.concatenate(sums, axis=1))
    mixture = (features[1] * features[2]).astype(BF16)
    query = features[0].astype(BF16)
    for n in range(count):

        @pl.when(step == n)
        def _():
            out_refs[n][...] = mixture
            out_refs[count + n][...] = query


def featurize(where, values, taps, halo, ctx_count, first, count):
    width, tokens = values.shape[1:]
    block = width // ctx_count
    lanes = max(block, 128)
    shape = jax.ShapeDtypeStruct((block, tokens), BF16)

    def rows(step, where_ref):
        return jnp.bitwise_xor(step + first, where_ref[0])

    def lanes_of(step, where_ref):
        return rows(step, where_ref) * block // lanes

    outs = pl.pallas_call(
        functools.partial(featurize_kernel, first, count),
        grid_spec=pltpu.PrefetchScalarGridSpec(
            num_scalar_prefetch=1,
            grid=(count,),
            in_specs=[
                pl.BlockSpec((3, block, tokens), lambda s, w: (0, rows(s, w), 0)),
                pl.BlockSpec((3, TAPS, lanes), lambda s, w: (0, 0, lanes_of(s, w))),
                pl.BlockSpec((halo.shape[0], lanes), lambda s, w: (0, lanes_of(s, w))),
            ],
            out_specs=[whole_spec(shape.shape)] * (2 * count),
            scratch_shapes=[pltpu.VMEM((lanes, 128), F32)] * 2,
        ),
        out_shape=[shape] * (2 * count),
        compiler_params=pltpu.CompilerParams(vmem_limit_bytes=32 * MIB),
        name="featurize",
    )(where, values, taps, halo)
    return outs[:count], outs[count:]


def convolve_kernel(ctx_count, where_ref, filters_ref, skip_ref, *refs):
    mixture_refs, out_refs = refs[:ctx_count], refs[ctx_count : 2 * ctx_count]
    left_ref, total_ref = refs[2 * ctx_count :]
    group = pl.program_id(0)
    me = where_ref[0]
    tokens = mixture_refs[0].shape[1]

    def rows_of(k):
        return pl.ds(pl.multiple_of(jnp.bitwise_xor(me, k) * GROUP, GROUP), GROUP)

    for k in range(ctx_count):
        left_ref[rows_of(k), :] = mixture_refs[k][...]
    total_ref[...] = jnp.zeros_like(total_ref)

    def add_lags(d, rows, taps):
        spread = jnp.broadcast_to(taps, (tokens, 2 * tokens))
        turned = pltpu.roll(spread, 0, 1, stride=1, stride_axis=0)[:, tokens:]
        product = jnp.dot(left_ref[:rows, :], turned.astype(BF16), preferred_element_type=F32)
        place = pl.ds(d * GROUP, rows)
        total_ref[place, :] = total_ref[place, :] + product

    zeros = jnp.zeros((1, tokens), F32)
    here = pl.ds(group, 1)
    first = jnp.concatenate([zeros, filters_ref[here, :tokens]], axis=1)
    add_lags(0, ctx_count * GROUP, first)
    if ctx_count <= 8:
        for d in range(1, ctx_count):
            lags = filters_ref[here, (d - 1) * tokens : (d + 1) * tokens]
            add_lags(d, (ctx_count - d) * GROUP, lags)
    else:

        @pl.loop(1, ctx_count)
        def _(d):
            start = pl.multiple_of((d - 1) * tokens, tokens)
            add_lags(d, ctx_count * GROUP, filters_ref[here, pl.ds(start, 2 * tokens)])

    skip = skip_ref[...]
    skip = jnp.concatenate([skip] * (tokens // 128), axis=1)
    for k in range(ctx_count):
        wide = mixture_refs[k][...].astype(F32)
        out_refs[k][...] = (total_ref[rows_of(k), :] + skip * wide).astype(BF16)


def convolve(where, filters, skip, mixtures):
    ctx_count = len(mixtures)
    block, tokens = mixtures[0].shape
    groups = filters.shape[0]
    total_rows = ctx_count * GROUP * (1 if ctx_count <= 8 else 2)
    rows = pl.BlockSpec((GROUP, tokens), lambda g, w: (g, 0))
    return pl.pallas_call(
        functools.partial(convolve_kernel, ctx_count),
        grid_spec=pltpu.PrefetchScalarGridSpec(
            num_scalar_prefetch=1,
            grid=(groups,),
            in_specs=[
                whole_spec(filters.shape),
                pl.BlockSpec((GROUP, 128), lambda g, w: (g, 0)),
            ]
            + [rows] * ctx_count,
            out_specs=[rows] * ctx_count,
            scratch_shapes=[
                pltpu.VMEM((ctx_count * GROUP, tokens), BF16),
                pltpu.VMEM((total_rows, tokens), F32),
            ],
        ),
        out_shape=[jax.ShapeDtypeStruct((block, tokens), BF16)] * ctx_count,
        compiler_params=pltpu.CompilerParams(vmem_limit_bytes=40 * MIB),
        name="convolve",
    )(where, filters, skip, *mixtures)


def gate_kernel(half, where_ref, query_ref, far_query_ref, summed_ref, far_summed_ref, out_ref):
    tokens = query_ref.shape[1]
    upper = (where_ref[0] >= half).astype(jnp.int32)
    near = query_ref[...].astype(F32) * summed_ref[...].astype(F32)
    far = far_query_ref[...].astype(F32) * far_summed_ref[...].astype(F32)
    near_place = pl.ds(pl.multiple_of(upper * tokens, tokens), tokens)
    far_place = pl.ds(pl.multiple_of((1 - upper) * tokens, tokens), tokens)
    out_ref[:, near_place] = near.astype(BF16)
    out_ref[:, far_place] = far.astype(BF16)


def gate(where, half, query, far_query, summed, far_summed):
    block, tokens = query.shape
    return pl.pallas_call(
        functools.partial(gate_kernel, half),
        grid_spec=pltpu.PrefetchScalarGridSpec(
            num_scalar_prefetch=1,
            grid=(1,),
            in_specs=[whole_spec((block, tokens))] * 4,
            out_specs=whole_spec((block, 2 * tokens)),
        ),
        out_shape=jax.ShapeDtypeStruct((block, 2 * tokens), BF16),
        compiler_params=pltpu.CompilerParams(vmem_limit_bytes=16 * MIB),
        name="gate",
    )(where, query, far_query, summed, far_summed)


def project_kernel(pieces, chunks, where_ref, *refs):
    weight_refs, gating_refs = refs[:pieces], refs[pieces : pieces + chunks]
    keep_ref, send_ref, gating_ref = refs[pieces + chunks :]
    me, low, core = where_ref[0], where_ref[1], where_ref[2]
    rows, width = weight_refs[0].shape
    block = width // chunks
    tile = min(rows, 256)
    for k in range(chunks):
        place = pl.ds(pl.multiple_of(jnp.bitwise_xor(me, k) * block, block), block)
        gating_ref[place, :] = gating_refs[k][...]
    for p in range(pieces):
        place = jnp.bitwise_xor(low, p)
        mine = (place >= pieces // 2).astype(jnp.int32) == core
        within = jnp.bitwise_and(place, pieces // 2 - 1) * rows

        @pl.loop(0, rows // tile)
        def _(r):
            start = pl.multiple_of(r * tile, tile)
            total = jnp.dot(
                weight_refs[p][pl.ds(start, tile), :],
                gating_ref[...],
                preferred_element_type=F32,
            )
            target = pl.ds(pl.multiple_of(within + start, tile), tile)

            @pl.when(mine)
            def _():
                keep_ref[target, :] = total

            @pl.when(jnp.logical_not(mine))
            def _():
                send_ref[target, :] = total


def project(where, weights, gatings):
    rows = weights[0].shape[0]
    tokens = gatings[0].shape[1]
    pieces = len(weights)
    out = jax.ShapeDtypeStruct((pieces // 2 * rows, tokens), F32)
    return pl.pallas_call(
        functools.partial(project_kernel, pieces, len(gatings)),
        grid_spec=pltpu.PrefetchScalarGridSpec(
            num_scalar_prefetch=1,
            grid=(1,),
            in_specs=[whole_spec(a.shape) for a in (*weights, *gatings)],
            out_specs=[whole_spec(out.shape)] * 2,
            scratch_shapes=[pltpu.VMEM((weights[0].shape[1], tokens), BF16)],
        ),
        out_shape=[out] * 2,
        compiler_params=pltpu.CompilerParams(vmem_limit_bytes=56 * MIB),
        name="project",
    )(where, *weights, *gatings)


def on_device(
    query_key_value_input,
    featurizer_weights,
    channel_skip_scale,
    group_long_filters,
    frozen_weight,
    down_update_weight,
    up_update_weight,
    magnitude,
):
    width, tokens = query_key_value_input.shape[1:]
    ctx_count = lax.axis_size("ctx")
    tp_count = lax.axis_size("tp")
    half = ctx_count // 2
    rows = frozen_weight.shape[0]
    me = lax.axis_index("ctx")
    tp_index = lax.axis_index("tp")
    low = jnp.bitwise_and(me, half - 1)
    high = me // half
    core = jnp.bitwise_and(tp_index, 1)
    upper_tp = tp_index // 2
    where = jnp.stack([me, low, core]).astype(jnp.int32)

    halo = jnp.swapaxes(query_key_value_input[:, :, tokens - (TAPS - 1) :], 1, 2)
    halo = halo.reshape(3 * (TAPS - 1), width)
    halo = lax.ppermute(halo, "ctx", [(i, i + 1) for i in range(ctx_count - 1)])

    update = jnp.dot(up_update_weight, down_update_weight, preferred_element_type=F32)
    merged = (frozen_weight.astype(F32) + update).astype(BF16)
    weights = [merged]
    norms = jnp.sum(jnp.square(lax.optimization_barrier(merged).astype(F32)), axis=1)[None, :]
    for distance in (1, 2):
        norms = norms + exchange(norms, "tp", distance)
    norms = [norms]
    distance = half // 2
    while distance:
        weights = weights + [exchange(piece, "ctx", distance) for piece in weights]
        norms = norms + [exchange(piece, "ctx", distance) for piece in norms]
        distance //= 2
    order = [0]
    distance = half // 2
    while distance:
        order = order + [index + distance for index in order]
        distance //= 2
    weights = [weights[order.index(p)] for p in range(half)]
    norms = [norms[order.index(p)] for p in range(half)]

    mixtures, queries = [], []
    for first in (0, half):
        some_mixtures, some_queries = featurize(
            where, query_key_value_input, featurizer_weights, halo, ctx_count, first, half
        )
        mixtures += some_mixtures
        queries += some_queries
    mixtures = mixtures[:1] + [exchange(mixtures[k], "ctx", k) for k in range(1, ctx_count)]
    queries = queries[:1] + [exchange(queries[k], "ctx", k) for k in range(1, ctx_count)]

    block = width // ctx_count
    skip = jnp.broadcast_to(channel_skip_scale[:, None], (block, 128))
    summed = convolve(where, group_long_filters, skip, mixtures)
    gatings = [
        gate(where, half, queries[m], queries[m + half], summed[m], summed[m + half])
        for m in range(half)
    ]
    gatings = [gatings[0]] + [
        exchange(gatings[k % half], "ctx", k) for k in range(1, ctx_count)
    ]
    keep, send = project(where, weights, gatings)
    partial = keep + exchange(send, "tp", 1)

    stacked = jnp.stack(norms).reshape(half, rows)
    stacked = stacked[jnp.bitwise_xor(jnp.arange(half), low)].reshape(half * rows)
    owned = half * rows // 2
    norms_here = lax.dynamic_slice_in_dim(stacked, core * owned, owned)
    magnitude_here = lax.dynamic_slice_in_dim(magnitude, (high * 2 + core) * owned, owned)
    scaling = magnitude_here / jnp.sqrt(norms_here + EPSILON)
    scaled = partial * scaling[:, None]
    near = lax.dynamic_slice_in_dim(scaled, high * tokens, tokens, axis=1)
    far = lax.dynamic_slice_in_dim(scaled, (1 - high) * tokens, tokens, axis=1)

    def place(h, l, y, c):
        return (h * half + l) * tp_count + y * 2 + c

    sites = [(h, l, c) for h in range(2) for l in range(half) for c in range(2)]
    both = ("ctx", "tp")
    from_near = lax.ppermute(
        near.astype(BF16),
        both,
        [(place(h, l, 1 - h, c), place(h, l, h, c)) for h, l, c in sites],
    )
    from_far = lax.ppermute(
        far.astype(BF16),
        both,
        [(place(h, l, h, c), place(1 - h, l, h, c)) for h, l, c in sites],
    )
    from_diagonal = lax.ppermute(
        far.astype(BF16),
        both,
        [(place(h, l, 1 - h, c), place(1 - h, l, h, c)) for h, l, c in sites],
    )
    own = jnp.where(upper_tp == high, near, from_far.astype(F32))
    other = jnp.where(upper_tp == high, from_near, from_diagonal).astype(F32)
    return (own + other).astype(BF16)


def solution(mesh):
    placed = (
        P(None, "tp", "ctx"),
        P(None, None, "tp"),
        P(("tp", "ctx")),
        P(("tp", "ctx"), None),
        P("ctx", "tp"),
        P(None, "tp"),
        P("ctx", None),
        P(),
    )
    return jax.shard_map(
        on_device, mesh=mesh, in_specs=placed, out_specs=P("tp", "ctx"), check_vma=False
    )
```

```python
import functools

import jax
import jax.numpy as jnp
from jax import lax
from jax.experimental import pallas as pl
from jax.experimental.pallas import tpu as pltpu
from jax.sharding import PartitionSpec as P

GROUP = 16
TAPS = 7
EPSILON = 1e-06
MIB = 1 << 20
VMEM_LIMIT = 24 * MIB
BF16 = jnp.bfloat16
F32 = jnp.float32


def exchange(block, axis, distance):
    count = lax.axis_size(axis)
    return lax.ppermute(block, axis, [(i, i ^ distance) for i in range(count)])


def whole_spec(shape):
    return pl.BlockSpec(shape, lambda *_: (0,) * len(shape))


def tail_kernel(input_ref, out_ref):
    rows = []
    for i in range(3):
        turned = input_ref[i].astype(F32).T
        rows.append(turned[turned.shape[0] - 8 :])
    rows.append(jnp.zeros_like(rows[0]))
    out_ref[...] = jnp.concatenate(rows, axis=0).astype(BF16)


def last_tokens(values):
    width, tokens = values.shape[1:]
    lanes = min(width, 512)
    return pl.pallas_call(
        tail_kernel,
        grid=(width // lanes,),
        in_specs=[pl.BlockSpec((3, lanes, 128), lambda c: (0, c, tokens // 128 - 1))],
        out_specs=pl.BlockSpec((32, lanes), lambda c: (0, c)),
        out_shape=jax.ShapeDtypeStruct((32, width), BF16),
        compiler_params=pltpu.CompilerParams(vmem_limit_bytes=VMEM_LIMIT),
        name="last_tokens",
    )(values)


def merge_kernel(cuts, frozen_ref, down_ref, up_ref, *refs):
    norms_ref, part_refs = refs[-1], refs[-1 - len(cuts) + 1 : -1]
    for part_ref, start, end in zip(part_refs, cuts, cuts[1:]):
        update = jnp.dot(up_ref[start:end, :], down_ref[...], preferred_element_type=F32)
        merged = (frozen_ref[start:end, :].astype(F32) + update).astype(BF16)
        part_ref[...] = merged
        squares = jnp.square(merged.astype(F32))
        norms_ref[start:end, :] = jnp.broadcast_to(
            jnp.sum(squares, axis=1, keepdims=True), (end - start, 128)
        )


def merge(cuts, frozen, down, up, *others):
    rows, width = frozen.shape
    return pl.pallas_call(
        functools.partial(merge_kernel, cuts),
        in_specs=[pl.BlockSpec(memory_space=pltpu.VMEM)] * 3
        + [pl.BlockSpec(memory_space=pl.ANY)] * len(others),
        out_shape=[
            jax.ShapeDtypeStruct((end - start, width), BF16) for start, end in zip(cuts, cuts[1:])
        ]
        + [jax.ShapeDtypeStruct((rows, 128), F32)],
        compiler_params=pltpu.CompilerParams(vmem_limit_bytes=VMEM_LIMIT),
        name="merge",
    )(frozen, down, up, *others)


def featurize_kernel(input_ref, taps_ref, halo_ref, mixture_ref, query_ref, held):
    block, tokens = input_ref.shape[1:]
    lanes = min(block, 128)
    shift = lax.rem(pl.program_id(0) * block, taps_ref.shape[2])
    for start in range(0, block, lanes):
        channels = slice(start, start + lanes)
        weights = []
        for i in range(3):
            taps = jnp.concatenate([taps_ref[i], jnp.zeros((1, taps_ref.shape[2]), F32)], axis=0)
            halo = halo_ref[...].astype(F32)[8 * i : 8 * i + 8]
            if block < 128:
                taps = pltpu.roll(taps, 128 - shift, 1)
                halo = pltpu.roll(halo, 128 - shift, 1)
            weights.append(taps[:, channels])
            held[i, :8, :] = halo[:, channels]
            held[i, 8:, :] = input_ref[i, channels, :].astype(F32).T
        for place in range(0, tokens, 128):
            sums = []
            for i in range(3):
                total = weights[i][0:1, :] * held[i, 8 + place : 136 + place, :]
                for j in range(1, TAPS):
                    total += weights[i][j : j + 1, :] * held[i, 8 + place - j : 136 + place - j, :]
                sums.append(total)
            here = (0, channels, slice(place, place + 128))
            mixture_ref[here] = (sums[1] * sums[2]).T.astype(BF16)
            query_ref[here] = sums[0].T.astype(BF16)


def featurize(values, taps, halo, ctx_count):
    width, tokens = values.shape[1:]
    block = width // ctx_count
    lanes = max(block, 128)
    shape = jax.ShapeDtypeStruct((ctx_count, block, tokens), BF16)
    out_spec = pl.BlockSpec((1, block, tokens), lambda d: (d, 0, 0))
    return pl.pallas_call(
        featurize_kernel,
        grid=(ctx_count,),
        in_specs=[
            pl.BlockSpec((3, block, tokens), lambda d: (0, d, 0)),
            pl.BlockSpec((3, TAPS, lanes), lambda d: (0, 0, d * block // lanes)),
            pl.BlockSpec((32, lanes), lambda d: (0, d * block // lanes)),
        ],
        out_specs=[out_spec] * 2,
        out_shape=[shape] * 2,
        scratch_shapes=[pltpu.VMEM((3, 8 + tokens, min(block, 128)), F32)],
        compiler_params=pltpu.CompilerParams(vmem_limit_bytes=VMEM_LIMIT),
        cost_estimate=pl.CostEstimate(
            flops=6 * TAPS * width * tokens, bytes_accessed=10 * MIB, transcendentals=0
        ),
        name="featurize",
    )(values, taps, halo)


def convolve_kernel(ctx_count, filters_ref, skip_ref, mixture_ref, added_ref, out_ref, total_ref):
    group = pl.program_id(0)
    tokens = mixture_ref.shape[2]

    @pl.when(group < filters_ref.shape[0])
    def _():
        left = mixture_ref[...].reshape(ctx_count * GROUP, tokens)

        def product(rows, taps):
            spread = jnp.broadcast_to(taps, (tokens, 2 * tokens))
            turned = pltpu.roll(spread, 0, 1, stride=1, stride_axis=0)[:, tokens:]
            return jnp.dot(left[:rows], turned.astype(BF16), preferred_element_type=F32)

        here = pl.ds(group, 1)
        first = jnp.concatenate([jnp.zeros((1, tokens), F32), filters_ref[here, :tokens]], axis=1)
        rows = ctx_count * GROUP
        total_ref[:rows, :] = product(rows, first)
        if ctx_count <= 8:
            for d in range(1, ctx_count):
                lags = filters_ref[here, (d - 1) * tokens : (d + 1) * tokens]
                total_ref[d * GROUP :, :] += product(rows - d * GROUP, lags)
        else:

            @pl.loop(1, ctx_count)
            def _(d):
                start = pl.multiple_of((d - 1) * tokens, tokens)
                place = pl.ds(pl.multiple_of(d * GROUP, GROUP), rows)
                lags = filters_ref[here, pl.ds(start, 2 * tokens)]
                total_ref[place, :] = total_ref[place, :] + product(rows, lags)

        skip = jnp.concatenate([skip_ref[...]] * (tokens // 128), axis=1)
        for j in range(ctx_count):
            wide = mixture_ref[j].astype(F32)
            total = total_ref[j * GROUP : (j + 1) * GROUP, :]
            out_ref[j] = (total + skip * wide).astype(BF16)

    @pl.when(group == filters_ref.shape[0])
    def _():
        for j in range(ctx_count):
            out_ref[j] = added_ref[...]


def convolve(filters, skip, mixture, added):
    ctx_count, block, tokens = mixture.shape
    groups = filters.shape[0]
    total_rows = ctx_count * GROUP * (1 if ctx_count <= 8 else 2)
    return pl.pallas_call(
        functools.partial(convolve_kernel, ctx_count),
        grid=(groups + 1,),
        in_specs=[
            whole_spec(filters.shape),
            pl.BlockSpec((GROUP, 128), lambda g: (jnp.minimum(g, groups - 1), 0)),
            pl.BlockSpec(
                (ctx_count, GROUP, tokens), lambda g: (0, jnp.minimum(g, groups - 1), 0)
            ),
            whole_spec(added.shape),
        ],
        out_specs=pl.BlockSpec((ctx_count, GROUP, tokens), lambda g: (0, g, 0)),
        scratch_shapes=[pltpu.VMEM((total_rows, tokens), F32)],
        out_shape=jax.ShapeDtypeStruct((ctx_count, block + GROUP, tokens), BF16),
        compiler_params=pltpu.CompilerParams(vmem_limit_bytes=VMEM_LIMIT),
        cost_estimate=pl.CostEstimate(
            flops=8 * block * (ctx_count * tokens) ** 2, bytes_accessed=20 * MIB, transcendentals=0
        ),
        name="convolve",
    )(filters, skip, mixture, added)


def gate_kernel(query_ref, summed_ref, out_ref):
    out_ref[...] = (query_ref[0].astype(F32) * summed_ref[0].astype(F32)).astype(BF16)


def gate(query, summed):
    ctx_count, block, tokens = query.shape
    spec = pl.BlockSpec((1, block, tokens), lambda d: (d, 0, 0))
    return pl.pallas_call(
        gate_kernel,
        grid=(ctx_count,),
        in_specs=[spec] * 2,
        out_specs=pl.BlockSpec((block, tokens), lambda d: (d, 0)),
        out_shape=jax.ShapeDtypeStruct((ctx_count * block, tokens), BF16),
        compiler_params=pltpu.CompilerParams(vmem_limit_bytes=VMEM_LIMIT),
        name="gate",
    )(query, summed)


def stage_kernel(*refs):
    *piece_refs, out_ref, sems = refs
    copies, at = [], 0
    for n, piece_ref in enumerate(piece_refs):
        rows = piece_ref.shape[0]
        copies.append(pltpu.make_async_copy(piece_ref, out_ref.at[pl.ds(at, rows), :], sems.at[n]))
        at += rows
    for copy in copies:
        copy.start()
    for copy in copies:
        copy.wait()


def stage_rows(pieces):
    rows = sum(piece.shape[0] for piece in pieces)
    return pl.pallas_call(
        stage_kernel,
        in_specs=[pl.BlockSpec(memory_space=pl.ANY)] * len(pieces),
        out_specs=pl.BlockSpec(memory_space=pltpu.VMEM),
        out_shape=jax.ShapeDtypeStruct((rows, pieces[0].shape[1]), BF16),
        scratch_shapes=[pltpu.SemaphoreType.DMA((len(pieces),))],
        compiler_params=pltpu.CompilerParams(vmem_limit_bytes=VMEM_LIMIT),
        name="stage_rows",
    )(*pieces)


def project_kernel(layout, places, where_ref, weight_ref, gating_ref, scaling_ref, *refs):
    keep_ref, send_ref = refs[-2:]
    low, core = where_ref[1], where_ref[2]
    tokens = keep_ref.shape[1]
    block = 2 * keep_ref.shape[0] // places
    total = jnp.dot(weight_ref[...], gating_ref[...], preferred_element_type=F32)
    at = 0
    for offset, rows, p in layout:
        place = jnp.bitwise_xor(low, p)
        mine = place // (places // 2) == core
        target = pl.ds(pl.multiple_of((place & (places // 2 - 1)) * block + offset, 16), rows)
        source = pl.ds(pl.multiple_of(place * block + offset, 16), rows)
        scaling = jnp.concatenate([scaling_ref[source, :]] * (tokens // 128), axis=1)
        scaled = total[at : at + rows] * scaling

        @pl.when(mine)
        def _():
            keep_ref[target, :] = scaled

        @pl.when(jnp.logical_not(mine))
        def _():
            send_ref[target, :] = scaled.astype(BF16)

        at += rows


def project(where, places, layout, weight, gating, scaling, *others):
    width, tokens = gating.shape
    total_rows = weight.shape[0]
    out = jax.ShapeDtypeStruct((total_rows // 2, tokens), F32)
    sent = jax.ShapeDtypeStruct((total_rows // 2, tokens), BF16)
    return pl.pallas_call(
        functools.partial(project_kernel, layout, places),
        grid_spec=pltpu.PrefetchScalarGridSpec(
            num_scalar_prefetch=1,
            grid=(1,),
            in_specs=[pl.BlockSpec(memory_space=pltpu.VMEM)] * 3
            + [pl.BlockSpec(memory_space=pl.ANY)] * len(others),
            out_specs=[pl.BlockSpec(memory_space=pltpu.VMEM)] * 2,
        ),
        out_shape=[out, sent],
        compiler_params=pltpu.CompilerParams(vmem_limit_bytes=28 * MIB),
        cost_estimate=pl.CostEstimate(
            flops=2 * total_rows * tokens * width, bytes_accessed=8 * MIB, transcendentals=0
        ),
        name="project",
    )(where, weight, gating, scaling, *others)


def after(value, *others):
    return lax.optimization_barrier((value, *others))[0]


def rows_with(norms, tokens):
    flat = norms.reshape(-1)
    flat = jnp.pad(flat, (0, -flat.shape[0] % tokens)).reshape(-1, tokens)
    pieces = []
    for _ in range(3):
        piece = lax.optimization_barrier(flat.astype(BF16))
        pieces.append(piece)
        flat = flat - piece.astype(F32)
    added = jnp.concatenate(pieces)
    return jnp.pad(added, ((0, GROUP - added.shape[0]), (0, 0)))


def norms_of(received, block, rows):
    ctx_count, _, tokens = received.shape
    lines = -(-rows // tokens)
    added = received[:, block : block + 3 * lines].astype(F32)
    added = added.reshape(ctx_count, 3, lines * tokens)
    return (added[:, 0] + (added[:, 1] + added[:, 2]))[:, :rows].reshape(ctx_count * rows)


def on_device(
    query_key_value_input,
    featurizer_weights,
    channel_skip_scale,
    group_long_filters,
    frozen_weight,
    down_update_weight,
    up_update_weight,
    magnitude,
):
    width, tokens = query_key_value_input.shape[1:]
    ctx_count = lax.axis_size("ctx")
    tp_count = lax.axis_size("tp")
    half = ctx_count // 2
    rows = frozen_weight.shape[0]
    me = lax.axis_index("ctx")
    tp_index = lax.axis_index("tp")
    low = jnp.bitwise_and(me, half - 1)
    high = me // half
    core = jnp.bitwise_and(tp_index, 1)
    upper_tp = tp_index // 2
    where = jnp.stack([me, low, core, high]).astype(jnp.int32)

    tail = last_tokens(query_key_value_input)
    halo = lax.ppermute(tail, "ctx", [(i, i + 1) for i in range(ctx_count - 1)])

    cuts = (0, rows * 3 // 8 // 16 * 16, rows * 5 // 8 // 16 * 16, rows)
    *parts, norms = merge(cuts, frozen_weight, down_update_weight, up_update_weight, tail)
    norms = norms[:, 0][None, :]
    norms = norms + sum(exchange(norms, "tp", distance) for distance in range(1, tp_count))

    taps = after(featurizer_weights, *parts)
    mixture, query = featurize(query_key_value_input, taps, halo, ctx_count)
    own_mixture = mixture
    mixture = lax.all_to_all(own_mixture, "ctx", split_axis=0, concat_axis=0, tiled=True)

    distances = []
    while 1 << len(distances) < half:
        distances.insert(0, 1 << len(distances))
    coarse, rest = distances[0], distances[1:]
    pieces, layout = [], []

    def finish(held, order, path, offset, length):
        for distance in path[:-1]:
            received = exchange(held, "ctx", distance)
            held = jnp.concatenate([held, received], axis=0)
            order = order + [index + distance for index in order]
        received = exchange(held, "ctx", path[-1])
        pieces.extend([held, received])
        layout.extend((offset, length, index) for index in order)
        layout.extend((offset, length, index + path[-1]) for index in order)
        return received

    part = after(parts[0], own_mixture)
    far_part = exchange(part, "ctx", coarse)
    got = finish(part, [0], rest, 0, cuts[1])
    block = width // ctx_count
    skip = jnp.broadcast_to(channel_skip_scale[:, None], (block, 128))
    summed = convolve(group_long_filters, skip, mixture, rows_with(norms, tokens))
    sent = after(summed, far_part, got)
    received = lax.all_to_all(sent, "ctx", split_axis=0, concat_axis=0, tiled=True)
    part = after(parts[1], sent)
    other_part = exchange(part, "ctx", coarse)
    got = finish(part, [0], rest, cuts[1], cuts[2] - cuts[1])
    gating = gate(after(query, received, got, other_part), received)
    far_gating = exchange(gating, "ctx", half)
    finish(after(far_part, gating), [coarse], rest, 0, cuts[1])
    finish(after(other_part, gating), [coarse], rest, cuts[1], cuts[2] - cuts[1])
    part = after(parts[2], gating)
    length = cuts[3] - cuts[2]
    if len(rest) == 1:
        upper = length // 3 // 16 * 16
        coarse_part, fine_part = exchange(part, "ctx", coarse), exchange(part, "ctx", rest[0])
        last = exchange(coarse_part[:upper], "ctx", rest[0])
        other = exchange(fine_part[upper:], "ctx", coarse)
        pieces.extend([part, coarse_part, fine_part, last, other])
        for index in (0, coarse, rest[0]):
            layout.append((cuts[2], length, index))
        layout.append((cuts[2], upper, coarse + rest[0]))
        layout.append((cuts[2] + upper, length - upper, coarse + rest[0]))
    else:
        finish(part, [0], distances, cuts[2], length)
    weight = stage_rows(pieces)

    first = high * half * rows
    norms_here = lax.dynamic_slice_in_dim(norms_of(received, block, rows), first, half * rows)
    magnitude_here = lax.dynamic_slice_in_dim(magnitude, first, half * rows)
    scaling = magnitude_here / jnp.sqrt(norms_here + EPSILON)
    scaling = jnp.broadcast_to(scaling[:, None], (half * rows, 128))

    def place(h, l, y, c):
        return (h * half + l) * tp_count + y * 2 + c

    sites = [(h, l, c) for h in range(2) for l in range(half) for c in range(2)]
    both = ("ctx", "tp")
    sums = []
    for gated in (gating, far_gating):
        keep, send = project(where, half, tuple(layout), weight, gated, scaling, *sums)
        sums.append((keep + exchange(send, "tp", 1).astype(F32)).astype(BF16))
    near, far = sums
    from_near = lax.ppermute(
        near, both, [(place(h, l, 1 - h, c), place(h, l, h, c)) for h, l, c in sites]
    )
    from_far = lax.ppermute(
        far, both, [(place(h, l, h, c), place(1 - h, l, h, c)) for h, l, c in sites]
    )
    from_diagonal = lax.ppermute(
        far, both, [(place(h, l, 1 - h, c), place(1 - h, l, h, c)) for h, l, c in sites]
    )
    own = jnp.where(upper_tp == high, near, from_far).astype(F32)
    other = jnp.where(upper_tp == high, from_near, from_diagonal).astype(F32)
    return (own + other).astype(BF16)


def solution(mesh):
    placed = (
        P(None, "tp", "ctx"),
        P(None, None, "tp"),
        P(("tp", "ctx")),
        P(("tp", "ctx"), None),
        P("ctx", "tp"),
        P(None, "tp"),
        P("ctx", None),
        P(),
    )
    return jax.shard_map(
        on_device, mesh=mesh, in_specs=placed, out_specs=P("tp", "ctx"), check_vma=False
    )
```

```python
import functools

import jax
import jax.numpy as jnp
from jax import lax
from jax.experimental import pallas as pl
from jax.experimental.pallas import tpu as pltpu
from jax.sharding import PartitionSpec as P

GROUP = 16
TAPS = 7
EPSILON = 1e-06
MIB = 1 << 20
VMEM_LIMIT = 24 * MIB
PROJECT_LIMIT = 56 * MIB
BF16 = jnp.bfloat16
F32 = jnp.float32


def exchange(block, axis, distance):
    count = lax.axis_size(axis)
    return lax.ppermute(block, axis, [(i, i ^ distance) for i in range(count)])


def whole_spec(shape):
    return pl.BlockSpec(shape, lambda *_: (0,) * len(shape))


def tail_kernel(input_ref, out_ref):
    rows = []
    for i in range(3):
        turned = input_ref[i].astype(F32).T
        rows.append(turned[turned.shape[0] - 8 :])
    rows.append(jnp.zeros_like(rows[0]))
    out_ref[...] = jnp.concatenate(rows, axis=0).astype(BF16)


def last_tokens(values):
    width, tokens = values.shape[1:]
    lanes = min(width, 512)
    return pl.pallas_call(
        tail_kernel,
        grid=(width // lanes,),
        in_specs=[pl.BlockSpec((3, lanes, 128), lambda c: (0, c, tokens // 128 - 1))],
        out_specs=pl.BlockSpec((32, lanes), lambda c: (0, c)),
        out_shape=jax.ShapeDtypeStruct((32, width), BF16),
        compiler_params=pltpu.CompilerParams(vmem_limit_bytes=VMEM_LIMIT),
        name="last_tokens",
    )(values)


def merge_kernel(cuts, frozen_ref, down_ref, up_ref, *refs):
    norms_ref, part_refs = refs[-1], refs[-1 - len(cuts) + 1 : -1]
    for part_ref, start, end in zip(part_refs, cuts, cuts[1:]):
        update = jnp.dot(up_ref[start:end, :], down_ref[...], preferred_element_type=F32)
        merged = (frozen_ref[start:end, :].astype(F32) + update).astype(BF16)
        part_ref[...] = merged
        squares = jnp.square(merged.astype(F32))
        norms_ref[start:end, :] = jnp.broadcast_to(
            jnp.sum(squares, axis=1, keepdims=True), (end - start, 128)
        )


def merge(cuts, frozen, down, up, *others):
    rows, width = frozen.shape
    return pl.pallas_call(
        functools.partial(merge_kernel, cuts),
        in_specs=[pl.BlockSpec(memory_space=pltpu.VMEM)] * 3
        + [pl.BlockSpec(memory_space=pl.ANY)] * len(others),
        out_shape=[
            jax.ShapeDtypeStruct((end - start, width), BF16) for start, end in zip(cuts, cuts[1:])
        ]
        + [jax.ShapeDtypeStruct((rows, 128), F32)],
        compiler_params=pltpu.CompilerParams(vmem_limit_bytes=VMEM_LIMIT),
        name="merge",
    )(frozen, down, up, *others)


def featurize_kernel(input_ref, taps_ref, halo_ref, mixture_ref, query_ref, held):
    block, tokens = mixture_ref.shape[1:]

    @pl.loop(0, input_ref.shape[1] // 128)
    def _(tile):
        channels = pl.ds(pl.multiple_of(tile * 128, 128), 128)
        weights = []
        for i in range(3):
            weights.append(taps_ref[i, :, channels])
            held[i, :8, :] = halo_ref[:, channels].astype(F32)[8 * i : 8 * i + 8]
            held[i, 8:, :] = input_ref[i, channels, :].T.astype(F32)
        for place in range(0, tokens, 128):
            sums = []
            for i in range(3):
                total = weights[i][0:1, :] * held[i, 8 + place : 136 + place, :]
                for j in range(1, TAPS):
                    total += weights[i][j : j + 1, :] * held[i, 8 + place - j : 136 + place - j, :]
                sums.append(total)
            columns = slice(place, place + 128)
            mixture = (sums[1] * sums[2]).astype(BF16).T
            query = sums[0].astype(BF16).T
            if block >= 128:
                rows = pl.ds(pl.multiple_of(lax.rem(tile * 128, block), 128), 128)
                mixture_ref[tile * 128 // block, rows, columns] = mixture
                query_ref[tile * 128 // block, rows, columns] = query
            else:
                for n in range(128 // block):
                    rows = slice(n * block, (n + 1) * block)
                    mixture_ref[tile * (128 // block) + n, :, columns] = mixture[rows]
                    query_ref[tile * (128 // block) + n, :, columns] = query[rows]


def featurize(values, taps, halo, ctx_count):
    width, tokens = values.shape[1:]
    shape = jax.ShapeDtypeStruct((ctx_count, width // ctx_count, tokens), BF16)
    return pl.pallas_call(
        featurize_kernel,
        in_specs=[pl.BlockSpec(memory_space=pltpu.VMEM)] * 3,
        out_specs=[pl.BlockSpec(memory_space=pltpu.VMEM)] * 2,
        out_shape=[shape] * 2,
        scratch_shapes=[pltpu.VMEM((3, 8 + tokens, 128), F32)],
        compiler_params=pltpu.CompilerParams(vmem_limit_bytes=VMEM_LIMIT),
        cost_estimate=pl.CostEstimate(
            flops=6 * TAPS * width * tokens, bytes_accessed=10 * MIB, transcendentals=0
        ),
        name="featurize",
    )(values, taps, halo)


def convolve_kernel(filters_ref, skip_ref, mixture_ref, added_ref, out_ref, total_ref):
    ctx_count, block, tokens = mixture_ref.shape
    rows = ctx_count * GROUP
    upper = lax.broadcasted_iota(jnp.int32, (tokens, tokens), 1) >= lax.broadcasted_iota(
        jnp.int32, (tokens, tokens), 0
    )

    @pl.loop(0, filters_ref.shape[0])
    def _(group):
        channels = pl.ds(pl.multiple_of(group * GROUP, GROUP), GROUP)
        here = pl.ds(group, 1)
        mixture = mixture_ref[:, channels, :]
        left = mixture.reshape(rows, tokens)

        def turned(start):
            taps = jnp.broadcast_to(filters_ref[here, pl.ds(start, tokens)], (tokens, tokens))
            return pltpu.roll(taps, 0, 1, stride=1, stride_axis=0)

        def product(count, these, before):
            matrix = jnp.where(upper, these, before).astype(BF16)
            return jnp.dot(left[:count], matrix, preferred_element_type=F32)

        before = turned(0)
        total_ref[:rows, :] = product(rows, before, 0.0)
        if ctx_count <= 8:
            for d in range(1, ctx_count):
                these = turned(d * tokens)
                total_ref[d * GROUP :, :] += product(rows - d * GROUP, these, before)
                before = these
        else:

            @pl.loop(1, ctx_count)
            def _(d):
                start = pl.multiple_of(d * tokens, tokens)
                place = pl.ds(pl.multiple_of(d * GROUP, GROUP), rows)
                matrices = turned(start), turned(start - tokens)
                total_ref[place, :] = total_ref[place, :] + product(rows, *matrices)

        skip = jnp.concatenate([skip_ref[channels, :]] * (tokens // 128), axis=1)
        for j in range(ctx_count):
            total = total_ref[j * GROUP : (j + 1) * GROUP, :]
            out_ref[j, channels, :] = (total + skip * mixture[j].astype(F32)).astype(BF16)

    for j in range(ctx_count):
        out_ref[j, block:, :] = added_ref[...]


def convolve(filters, skip, mixture, added):
    ctx_count, block, tokens = mixture.shape
    total_rows = ctx_count * GROUP * (1 if ctx_count <= 8 else 2)
    return pl.pallas_call(
        convolve_kernel,
        in_specs=[pl.BlockSpec(memory_space=pltpu.VMEM)] * 4,
        out_specs=pl.BlockSpec(memory_space=pltpu.VMEM),
        scratch_shapes=[pltpu.VMEM((total_rows, tokens), F32)],
        out_shape=jax.ShapeDtypeStruct((ctx_count, block + GROUP, tokens), BF16),
        compiler_params=pltpu.CompilerParams(vmem_limit_bytes=VMEM_LIMIT),
        cost_estimate=pl.CostEstimate(
            flops=8 * block * (ctx_count * tokens) ** 2, bytes_accessed=20 * MIB, transcendentals=0
        ),
        name="convolve",
    )(filters, skip, mixture, added)


def gate_kernel(query_ref, summed_ref, out_ref):
    ctx_count, block = query_ref.shape[:2]
    for d in range(ctx_count):
        product = query_ref[d].astype(F32) * summed_ref[d, :block, :].astype(F32)
        out_ref[d * block : (d + 1) * block, :] = product.astype(BF16)


def gate(query, summed):
    ctx_count, block, tokens = query.shape
    return pl.pallas_call(
        gate_kernel,
        in_specs=[pl.BlockSpec(memory_space=pltpu.VMEM)] * 2,
        out_specs=pl.BlockSpec(memory_space=pltpu.VMEM),
        out_shape=jax.ShapeDtypeStruct((ctx_count * block, tokens), BF16),
        compiler_params=pltpu.CompilerParams(vmem_limit_bytes=VMEM_LIMIT),
        name="gate",
    )(query, summed)


def project_kernel(layout, places, where_ref, gating_ref, far_gating_ref, *refs):
    arrays = len(layout)
    weight_refs = refs[:arrays]
    keep_refs, far_keep_refs = refs[arrays : arrays + 2]
    send_ref, held, gating_held, sems = refs[arrays + 2 :]
    low, core = where_ref[1], where_ref[2]
    tokens = gating_ref.shape[1]
    block = 2 * keep_refs.shape[0] // places
    copies, at = [], 0
    for n, source in enumerate((gating_ref, far_gating_ref)):
        target = gating_held.at[:, pl.ds(n * tokens, tokens)]
        copies.append(pltpu.make_async_copy(source, target, sems.at[n]))
    for n, weight_ref in enumerate(weight_refs):
        rows = weight_ref.shape[0]
        target = held.at[pl.ds(at, rows), :]
        copies.append(pltpu.make_async_copy(weight_ref, target, sems.at[n + 2]))
        at += rows
    for copy in copies:
        copy.start()
    copies[0].wait()
    copies[1].wait()
    pending, first, at = [], 0, 0
    total_rows = held.shape[0]
    for n, (copy, entries) in enumerate(zip(copies[2:], layout)):
        copy.wait()
        for entry in entries:
            pending.append((at, entry))
            at += entry[1]
        if at - first < total_rows // 4 and n + 1 < arrays:
            continue
        total = jnp.dot(held[first:at, :], gating_held[...], preferred_element_type=F32)
        for begin, (offset, rows, p) in pending:
            place = jnp.bitwise_xor(low, p)
            mine = place // (places // 2) == core
            start = (place & (places // 2 - 1)) * block + offset
            target = pl.ds(pl.multiple_of(start, 16), rows)
            piece = total[begin - first : begin - first + rows]

            @pl.when(mine)
            def _():
                keep_refs[target, :] = piece[:, :tokens]
                far_keep_refs[target, :] = piece[:, tokens:]

            @pl.when(jnp.logical_not(mine))
            def _():
                send_ref[0, target, :] = piece[:, :tokens].astype(BF16)
                send_ref[1, target, :] = piece[:, tokens:].astype(BF16)

        pending, first = [], at


def project(where, places, layout, weights, gating, far_gating):
    width, tokens = gating.shape
    total_rows = sum(weight.shape[0] for weight in weights)
    out = jax.ShapeDtypeStruct((total_rows // 2, tokens), F32)
    sent = jax.ShapeDtypeStruct((2, total_rows // 2, tokens), BF16)
    return pl.pallas_call(
        functools.partial(project_kernel, layout, places),
        grid_spec=pltpu.PrefetchScalarGridSpec(
            num_scalar_prefetch=1,
            grid=(1,),
            in_specs=[pl.BlockSpec(memory_space=pl.ANY)] * (2 + len(weights)),
            out_specs=[pl.BlockSpec(memory_space=pltpu.VMEM)] * 3,
            scratch_shapes=[
                pltpu.VMEM((total_rows, width), BF16),
                pltpu.VMEM((width, 2 * tokens), BF16),
                pltpu.SemaphoreType.DMA((len(weights) + 2,)),
            ],
        ),
        out_shape=[out, out, sent],
        compiler_params=pltpu.CompilerParams(vmem_limit_bytes=PROJECT_LIMIT),
        cost_estimate=pl.CostEstimate(
            flops=4 * total_rows * tokens * width, bytes_accessed=10 * MIB, transcendentals=0
        ),
        name="project",
    )(where, gating, far_gating, *weights)


def after(value, *others):
    return lax.optimization_barrier((value, *others))[0]


def rows_with(norms, tokens):
    flat = norms.reshape(-1)
    flat = jnp.pad(flat, (0, -flat.shape[0] % tokens)).reshape(-1, tokens)
    pieces = []
    for _ in range(3):
        piece = lax.optimization_barrier(flat.astype(BF16))
        pieces.append(piece)
        flat = flat - piece.astype(F32)
    added = jnp.concatenate(pieces)
    return jnp.pad(added, ((0, GROUP - added.shape[0]), (0, 0)))


def norms_of(received, block, rows):
    ctx_count, _, tokens = received.shape
    lines = -(-rows // tokens)
    added = received[:, block : block + 3 * lines].astype(F32)
    added = added.reshape(ctx_count, 3, lines * tokens)
    return (added[:, 0] + (added[:, 1] + added[:, 2]))[:, :rows].reshape(ctx_count * rows)


def on_device(
    query_key_value_input,
    featurizer_weights,
    channel_skip_scale,
    group_long_filters,
    frozen_weight,
    down_update_weight,
    up_update_weight,
    magnitude,
):
    width, tokens = query_key_value_input.shape[1:]
    ctx_count = lax.axis_size("ctx")
    tp_count = lax.axis_size("tp")
    half = ctx_count // 2
    rows = frozen_weight.shape[0]
    me = lax.axis_index("ctx")
    tp_index = lax.axis_index("tp")
    low = jnp.bitwise_and(me, half - 1)
    high = me // half
    core = jnp.bitwise_and(tp_index, 1)
    upper_tp = tp_index // 2
    where = jnp.stack([me, low, core, high]).astype(jnp.int32)

    tail = last_tokens(query_key_value_input)
    halo = lax.ppermute(tail, "ctx", [(i, i + 1) for i in range(ctx_count - 1)])

    mixture, query = featurize(query_key_value_input, featurizer_weights, halo, ctx_count)
    own_mixture = mixture
    mixture = lax.all_to_all(own_mixture, "ctx", split_axis=0, concat_axis=0, tiled=True)

    cuts = (0, rows * 3 // 8 // 16 * 16, rows * 5 // 8 // 16 * 16, rows)
    frozen = after(frozen_weight, own_mixture)
    *parts, norms = merge(cuts, frozen, down_update_weight, up_update_weight)
    norms = norms[:, 0][None, :]
    norms = norms + sum(exchange(norms, "tp", distance) for distance in range(1, tp_count))

    distances = []
    while 1 << len(distances) < half:
        distances.insert(0, 1 << len(distances))
    coarse, rest = distances[0], distances[1:]
    pieces, layout = [], []

    def finish(held, order, path, offset, length):
        for distance in path[:-1]:
            received = exchange(held, "ctx", distance)
            held = jnp.concatenate([held, received], axis=0)
            order = order + [index + distance for index in order]
        received = exchange(held, "ctx", path[-1])
        pieces.extend([held, received])
        layout.append(tuple((offset, length, index) for index in order))
        layout.append(tuple((offset, length, index + path[-1]) for index in order))
        return received

    part = parts[0]
    far_part = exchange(part, "ctx", coarse)
    got = finish(part, [0], rest, 0, cuts[1])
    block = width // ctx_count
    skip = jnp.broadcast_to(channel_skip_scale[:, None], (block, 128))
    summed = convolve(group_long_filters, skip, mixture, rows_with(norms, tokens))
    sent = after(summed, far_part, got)
    received = lax.all_to_all(sent, "ctx", split_axis=0, concat_axis=0, tiled=True)
    part = after(parts[1], sent)
    other_part = exchange(part, "ctx", coarse)
    got = finish(part, [0], rest, cuts[1], cuts[2] - cuts[1])
    gating = gate(after(query, received, got, other_part), received)
    far_gating = exchange(gating, "ctx", half)
    owned = half * rows // 2
    norms_here = norms_of(after(received, gating), block, rows)
    norms_here = lax.dynamic_slice_in_dim(norms_here, tp_index * owned, owned)
    magnitude_here = lax.dynamic_slice_in_dim(magnitude, tp_index * owned, owned)
    scaling = magnitude_here / jnp.sqrt(norms_here + EPSILON)

    finish(after(far_part, scaling), [coarse], rest, 0, cuts[1])
    finish(after(other_part, scaling), [coarse], rest, cuts[1], cuts[2] - cuts[1])
    part = after(parts[2], scaling)
    late_start, late_rows = cuts[2], cuts[3] - cuts[2]
    if len(rest) == 1:
        upper = late_rows // 3 // 16 * 16
        coarse_part, fine_part = exchange(part, "ctx", coarse), exchange(part, "ctx", rest[0])
        last = exchange(coarse_part[:upper], "ctx", rest[0])
        other = exchange(fine_part[upper:], "ctx", coarse)
        pieces += [part, coarse_part, fine_part, last, other]
        layout += [((late_start, late_rows, index),) for index in (0, coarse, rest[0])]
        layout.append(((late_start, upper, coarse + rest[0]),))
        layout.append(((late_start + upper, late_rows - upper, coarse + rest[0]),))
    else:
        finish(part, [0], distances, late_start, late_rows)
    layout = tuple(layout)

    def place(h, l, y, c):
        return (h * half + l) * tp_count + y * 2 + c

    sites = [(h, l, c) for h in range(2) for l in range(half) for c in range(2)]

    def send_on(value, route):
        pairs = [route(h, l, c) for h, l, c in sites]
        return lax.ppermute(value, ("ctx", "tp"), [(place(*a), place(*b)) for a, b in pairs])

    near, far, sent = project(where, half, layout, pieces, gating, far_gating)
    received = exchange(sent, "tp", 1).astype(F32)
    far = far + received[1]
    split = owned // 2
    mine = lax.dynamic_slice_in_dim(far, upper_tp * split, split)
    theirs = lax.dynamic_slice_in_dim(far, (1 - upper_tp) * split, split).astype(BF16)
    far = (mine + exchange(theirs, "tp", 2).astype(F32)).astype(BF16)
    straight = send_on(far, lambda h, l, c: ((h, l, h, c), (1 - h, l, h, c)))
    diagonal = send_on(far, lambda h, l, c: ((h, l, 1 - h, c), (1 - h, l, h, c)))
    near = (near + received[0]).astype(BF16)
    from_near = send_on(near, lambda h, l, c: ((h, l, 1 - h, c), (h, l, h, c)))
    from_far = jnp.where(
        upper_tp == 0,
        jnp.concatenate([straight, diagonal], axis=0),
        jnp.concatenate([diagonal, straight], axis=0),
    )
    near = near.astype(F32) + from_near.astype(F32)
    out = jnp.where(upper_tp == high, near, from_far.astype(F32))
    return (out * scaling[:, None]).astype(BF16)


def solution(mesh):
    placed = (
        P(None, "tp", "ctx"),
        P(None, None, "tp"),
        P(("tp", "ctx")),
        P(("tp", "ctx"), None),
        P("ctx", "tp"),
        P(None, "tp"),
        P("ctx", None),
        P(),
    )
    return jax.shard_map(
        on_device, mesh=mesh, in_specs=placed, out_specs=P("tp", "ctx"), check_vma=False
    )
```

```python
import functools
import math

import jax
import jax.numpy as jnp
from jax import lax
from jax.experimental import pallas as pl
from jax.experimental.pallas import tpu as pltpu
from jax.sharding import PartitionSpec as P

GROUP = 16
TAPS = 7
EPSILON = 1e-06
MIB = 1 << 20
VMEM_LIMIT = 24 * MIB
PROJECT_LIMIT = 56 * MIB
BF16 = jnp.bfloat16
F32 = jnp.float32


def exchange(block, axis, distance):
    count = lax.axis_size(axis)
    return lax.ppermute(block, axis, [(i, i ^ distance) for i in range(count)])


def whole_spec(shape):
    return pl.BlockSpec(shape, lambda *_: (0,) * len(shape))


def tail_kernel(input_ref, out_ref):
    rows = []
    for i in range(3):
        turned = input_ref[i].astype(F32).T
        rows.append(turned[turned.shape[0] - 8 :])
    rows.append(jnp.zeros_like(rows[0]))
    out_ref[...] = jnp.concatenate(rows, axis=0).astype(BF16)


def last_tokens(values):
    width, tokens = values.shape[1:]
    lanes = min(width, 512)
    return pl.pallas_call(
        tail_kernel,
        grid=(width // lanes,),
        in_specs=[pl.BlockSpec((3, lanes, 128), lambda c: (0, c, tokens // 128 - 1))],
        out_specs=pl.BlockSpec((32, lanes), lambda c: (0, c)),
        out_shape=jax.ShapeDtypeStruct((32, width), BF16),
        compiler_params=pltpu.CompilerParams(vmem_limit_bytes=VMEM_LIMIT),
        name="last_tokens",
    )(values)


def merge_kernel(cuts, frozen_ref, down_ref, up_ref, *refs):
    norms_ref, part_refs = refs[-1], refs[-1 - len(cuts) + 1 : -1]
    for part_ref, start, end in zip(part_refs, cuts, cuts[1:]):
        update = jnp.dot(up_ref[start:end, :], down_ref[...], preferred_element_type=F32)
        merged = (frozen_ref[start:end, :].astype(F32) + update).astype(BF16)
        part_ref[...] = merged
        squares = jnp.square(merged.astype(F32))
        norms_ref[start:end, :] = jnp.broadcast_to(
            jnp.sum(squares, axis=1, keepdims=True), (end - start, 128)
        )


def merge(cuts, frozen, down, up, *others):
    rows, width = frozen.shape
    return pl.pallas_call(
        functools.partial(merge_kernel, cuts),
        in_specs=[pl.BlockSpec(memory_space=pltpu.VMEM)] * 3
        + [pl.BlockSpec(memory_space=pl.ANY)] * len(others),
        out_shape=[
            jax.ShapeDtypeStruct((end - start, width), BF16) for start, end in zip(cuts, cuts[1:])
        ]
        + [jax.ShapeDtypeStruct((rows, 128), F32)],
        compiler_params=pltpu.CompilerParams(vmem_limit_bytes=VMEM_LIMIT),
        name="merge",
    )(frozen, down, up, *others)


def featurize_kernel(input_ref, taps_ref, halo_ref, mixture_ref, query_ref, held):
    block, tokens = mixture_ref.shape[1:]

    @pl.loop(0, input_ref.shape[1] // 128, unroll=math.gcd(4, input_ref.shape[1] // 128))
    def _(tile):
        channels = pl.ds(pl.multiple_of(tile * 128, 128), 128)
        weights = []
        for i in range(3):
            weights.append(taps_ref[i, :, channels])
            held[i, :8, :] = halo_ref[:, channels].astype(F32)[8 * i : 8 * i + 8]
            held[i, 8:, :] = input_ref[i, channels, :].T.astype(F32)
        for place in range(0, tokens, 128):
            sums = []
            for i in range(3):
                total = weights[i][0:1, :] * held[i, 8 + place : 136 + place, :]
                for j in range(1, TAPS):
                    total += weights[i][j : j + 1, :] * held[i, 8 + place - j : 136 + place - j, :]
                sums.append(total)
            columns = slice(place, place + 128)
            mixture = (sums[1] * sums[2]).astype(BF16).T
            query = sums[0].astype(BF16).T
            if block >= 128:
                rows = pl.ds(pl.multiple_of(lax.rem(tile * 128, block), 128), 128)
                mixture_ref[tile * 128 // block, rows, columns] = mixture
                query_ref[tile * 128 // block, rows, columns] = query
            else:
                for n in range(128 // block):
                    rows = slice(n * block, (n + 1) * block)
                    mixture_ref[tile * (128 // block) + n, :, columns] = mixture[rows]
                    query_ref[tile * (128 // block) + n, :, columns] = query[rows]


def featurize(values, taps, halo, ctx_count):
    width, tokens = values.shape[1:]
    shape = jax.ShapeDtypeStruct((ctx_count, width // ctx_count, tokens), BF16)
    return pl.pallas_call(
        featurize_kernel,
        in_specs=[pl.BlockSpec(memory_space=pltpu.VMEM)] * 3,
        out_specs=[pl.BlockSpec(memory_space=pltpu.VMEM)] * 2,
        out_shape=[shape] * 2,
        scratch_shapes=[pltpu.VMEM((3, 8 + tokens, 128), F32)],
        compiler_params=pltpu.CompilerParams(vmem_limit_bytes=VMEM_LIMIT),
        cost_estimate=pl.CostEstimate(
            flops=6 * TAPS * width * tokens, bytes_accessed=10 * MIB, transcendentals=0
        ),
        name="featurize",
    )(values, taps, halo)


def convolve_kernel(filters_ref, skip_ref, mixture_ref, added_ref, result_ref, total_ref, out_ref, sems):
    ctx_count, block, tokens = mixture_ref.shape
    rows = ctx_count * GROUP

    def copy_out(group):
        place = (slice(None), pl.ds(pl.multiple_of(group * GROUP, GROUP), GROUP))
        return pltpu.make_async_copy(out_ref.at[place], result_ref.at[place], sems.at[group])

    for j in range(ctx_count):
        out_ref[j, block:, :] = added_ref[...]
    copy_out(block // GROUP).start()
    upper = lax.broadcasted_iota(jnp.int32, (tokens, tokens), 1) >= lax.broadcasted_iota(
        jnp.int32, (tokens, tokens), 0
    )

    @pl.loop(0, filters_ref.shape[0], unroll=math.gcd(4, filters_ref.shape[0]))
    def _(group):
        channels = pl.ds(pl.multiple_of(group * GROUP, GROUP), GROUP)
        here = pl.ds(group, 1)
        mixture = mixture_ref[:, channels, :]
        left = mixture.reshape(rows, tokens)

        def turned(start):
            taps = jnp.broadcast_to(filters_ref[here, pl.ds(start, tokens)], (tokens, tokens))
            return pltpu.roll(taps, 0, 1, stride=1, stride_axis=0)

        def product(count, these, before):
            matrix = jnp.where(upper, these, before).astype(BF16)
            return jnp.dot(left[:count], matrix, preferred_element_type=F32)

        before = turned(0)
        total_ref[:rows, :] = product(rows, before, 0.0)
        if ctx_count <= 8:
            for d in range(1, ctx_count):
                these = turned(d * tokens)
                total_ref[d * GROUP :, :] += product(rows - d * GROUP, these, before)
                before = these
        else:

            @pl.loop(1, ctx_count)
            def _(d):
                start = pl.multiple_of(d * tokens, tokens)
                place = pl.ds(pl.multiple_of(d * GROUP, GROUP), rows)
                matrices = turned(start), turned(start - tokens)
                total_ref[place, :] = total_ref[place, :] + product(rows, *matrices)

        skip = jnp.concatenate([skip_ref[channels, :]] * (tokens // 128), axis=1)
        for j in range(ctx_count):
            total = total_ref[j * GROUP : (j + 1) * GROUP, :]
            out_ref[j, channels, :] = (total + skip * mixture[j].astype(F32)).astype(BF16)
        copy_out(group).start()

    @pl.loop(0, block // GROUP + 1)
    def _(group):
        copy_out(group).wait()


def convolve(filters, skip, mixture, added):
    ctx_count, block, tokens = mixture.shape
    total_rows = ctx_count * GROUP * (1 if ctx_count <= 8 else 2)
    return pl.pallas_call(
        convolve_kernel,
        in_specs=[pl.BlockSpec(memory_space=pltpu.VMEM)] * 4,
        out_specs=pl.BlockSpec(memory_space=pl.ANY),
        scratch_shapes=[
            pltpu.VMEM((total_rows, tokens), F32),
            pltpu.VMEM((ctx_count, block + GROUP, tokens), BF16),
            pltpu.SemaphoreType.DMA((block // GROUP + 1,)),
        ],
        out_shape=jax.ShapeDtypeStruct((ctx_count, block + GROUP, tokens), BF16),
        compiler_params=pltpu.CompilerParams(vmem_limit_bytes=VMEM_LIMIT),
        cost_estimate=pl.CostEstimate(
            flops=8 * block * (ctx_count * tokens) ** 2, bytes_accessed=20 * MIB, transcendentals=0
        ),
        name="convolve",
    )(filters, skip, mixture, added)


def gate_kernel(query_ref, summed_ref, out_ref):
    ctx_count, block = query_ref.shape[:2]
    for d in range(ctx_count):
        product = query_ref[d].astype(F32) * summed_ref[d, :block, :].astype(F32)
        out_ref[d * block : (d + 1) * block, :] = product.astype(BF16)


def gate(query, summed):
    ctx_count, block, tokens = query.shape
    return pl.pallas_call(
        gate_kernel,
        in_specs=[pl.BlockSpec(memory_space=pltpu.VMEM)] * 2,
        out_specs=pl.BlockSpec(memory_space=pltpu.VMEM),
        out_shape=jax.ShapeDtypeStruct((ctx_count * block, tokens), BF16),
        compiler_params=pltpu.CompilerParams(vmem_limit_bytes=VMEM_LIMIT),
        name="gate",
    )(query, summed)


def project_kernel(layout, places, where_ref, gating_ref, far_gating_ref, *refs):
    arrays = len(layout)
    weight_refs = refs[:arrays]
    keep_refs, far_keep_refs, send_ref = refs[arrays : arrays + 3]
    held, gating_held, kept, sent, sems, out_sems = refs[arrays + 3 :]
    low, core = where_ref[1], where_ref[2]
    tokens = gating_ref.shape[1]
    block = 2 * keep_refs.shape[0] // places
    copies, at = [], 0
    for n, source in enumerate((gating_ref, far_gating_ref)):
        target = gating_held.at[:, pl.ds(n * tokens, tokens)]
        copies.append(pltpu.make_async_copy(source, target, sems.at[n]))
    for n, weight_ref in enumerate(weight_refs):
        rows = weight_ref.shape[0]
        target = held.at[pl.ds(at, rows), :]
        copies.append(pltpu.make_async_copy(weight_ref, target, sems.at[n + 2]))
        at += rows
    for copy in copies:
        copy.start()
    copies[0].wait()
    copies[1].wait()
    pending, outs, first, at = [], [], 0, 0
    total_rows = held.shape[0]
    for n, (copy, entries) in enumerate(zip(copies[2:], layout)):
        copy.wait()
        for entry in entries:
            pending.append((at, entry))
            at += entry[1]
        if at - first < (total_rows // 4 if first else total_rows // 8) and n + 1 < arrays:
            continue
        total = jnp.dot(held[first:at, :], gating_held[...], preferred_element_type=F32)
        for begin, (offset, rows, p) in pending:
            place = jnp.bitwise_xor(low, p)
            mine = place // (places // 2) == core
            start = (place & (places // 2 - 1)) * block + offset
            target = pl.ds(pl.multiple_of(start, 16), rows)
            piece = total[begin - first : begin - first + rows]
            here = slice(begin, begin + rows)
            sem = [out_sems.at[len(outs), n] for n in range(2)]
            keeping = [
                pltpu.make_async_copy(kept.at[0, here, :], keep_refs.at[target, :], sem[0]),
                pltpu.make_async_copy(kept.at[1, here, :], far_keep_refs.at[target, :], sem[1]),
            ]
            sending = [
                pltpu.make_async_copy(sent.at[n, here, :], send_ref.at[n, target, :], sem[n])
                for n in range(2)
            ]
            outs.append((mine, keeping, sending))

            @pl.when(mine)
            def _():
                for n in range(2):
                    kept[n, here, :] = piece[:, n * tokens : (n + 1) * tokens]
                    keeping[n].start()

            @pl.when(jnp.logical_not(mine))
            def _():
                for n in range(2):
                    sent[n, here, :] = piece[:, n * tokens : (n + 1) * tokens].astype(BF16)
                    sending[n].start()

        pending, first = [], at
    for mine, keeping, sending in outs:

        @pl.when(mine)
        def _():
            for copy in keeping:
                copy.wait()

        @pl.when(jnp.logical_not(mine))
        def _():
            for copy in sending:
                copy.wait()


def project(where, places, layout, weights, gating, far_gating):
    width, tokens = gating.shape
    total_rows = sum(weight.shape[0] for weight in weights)
    out = jax.ShapeDtypeStruct((total_rows // 2, tokens), F32)
    sent = jax.ShapeDtypeStruct((2, total_rows // 2, tokens), BF16)
    return pl.pallas_call(
        functools.partial(project_kernel, layout, places),
        grid_spec=pltpu.PrefetchScalarGridSpec(
            num_scalar_prefetch=1,
            grid=(1,),
            in_specs=[pl.BlockSpec(memory_space=pl.ANY)] * (2 + len(weights)),
            out_specs=[pl.BlockSpec(memory_space=pl.ANY)] * 3,
            scratch_shapes=[
                pltpu.VMEM((total_rows, width), BF16),
                pltpu.VMEM((width, 2 * tokens), BF16),
                pltpu.VMEM((2, total_rows, tokens), F32),
                pltpu.VMEM((2, total_rows, tokens), BF16),
                pltpu.SemaphoreType.DMA((len(weights) + 2,)),
                pltpu.SemaphoreType.DMA((sum(map(len, layout)), 2)),
            ],
        ),
        out_shape=[out, out, sent],
        compiler_params=pltpu.CompilerParams(vmem_limit_bytes=PROJECT_LIMIT),
        cost_estimate=pl.CostEstimate(
            flops=4 * total_rows * tokens * width, bytes_accessed=10 * MIB, transcendentals=0
        ),
        name="project",
    )(where, gating, far_gating, *weights)


def after(value, *others):
    return lax.optimization_barrier((value, *others))[0]


def rows_with(norms, tokens):
    flat = norms.reshape(-1)
    flat = jnp.pad(flat, (0, -flat.shape[0] % tokens)).reshape(-1, tokens)
    pieces = []
    for _ in range(3):
        piece = lax.optimization_barrier(flat.astype(BF16))
        pieces.append(piece)
        flat = flat - piece.astype(F32)
    added = jnp.concatenate(pieces)
    return jnp.pad(added, ((0, GROUP - added.shape[0]), (0, 0)))


def norms_of(received, block, rows):
    ctx_count, _, tokens = received.shape
    lines = -(-rows // tokens)
    added = received[:, block : block + 3 * lines].astype(F32)
    added = added.reshape(ctx_count, 3, lines * tokens)
    return (added[:, 0] + (added[:, 1] + added[:, 2]))[:, :rows].reshape(ctx_count * rows)


def on_device(
    query_key_value_input,
    featurizer_weights,
    channel_skip_scale,
    group_long_filters,
    frozen_weight,
    down_update_weight,
    up_update_weight,
    magnitude,
):
    width, tokens = query_key_value_input.shape[1:]
    ctx_count = lax.axis_size("ctx")
    tp_count = lax.axis_size("tp")
    half = ctx_count // 2
    rows = frozen_weight.shape[0]
    me = lax.axis_index("ctx")
    tp_index = lax.axis_index("tp")
    low = jnp.bitwise_and(me, half - 1)
    high = me // half
    core = jnp.bitwise_and(tp_index, 1)
    upper_tp = tp_index // 2
    where = jnp.stack([me, low, core, high]).astype(jnp.int32)

    tail = last_tokens(query_key_value_input)
    halo = lax.ppermute(tail, "ctx", [(i, i + 1) for i in range(ctx_count - 1)])

    mixture, query = featurize(query_key_value_input, featurizer_weights, halo, ctx_count)
    own_mixture = mixture
    mixture = lax.all_to_all(own_mixture, "ctx", split_axis=0, concat_axis=0, tiled=True)

    cuts = (0, rows * 12 // 32 // 16 * 16, rows * 21 // 32 // 16 * 16, rows)
    frozen = after(frozen_weight, own_mixture)
    *parts, norms = merge(cuts, frozen, down_update_weight, up_update_weight)
    norms = norms[:, 0][None, :]
    norms = norms + sum(exchange(norms, "tp", distance) for distance in range(1, tp_count))

    distances = []
    while 1 << len(distances) < half:
        distances.insert(0, 1 << len(distances))
    coarse, rest = distances[0], distances[1:]
    pieces, layout = [], []

    def finish(held, order, path, offset, length):
        for distance in path[:-1]:
            received = exchange(held, "ctx", distance)
            held = jnp.concatenate([held, received], axis=0)
            order = order + [index + distance for index in order]
        received = exchange(held, "ctx", path[-1])
        pieces.extend([held, received])
        layout.append(tuple((offset, length, index) for index in order))
        layout.append(tuple((offset, length, index + path[-1]) for index in order))
        return received

    part = parts[0]
    far_part = exchange(part, "ctx", coarse)
    got = finish(part, [0], rest, 0, cuts[1])
    block = width // ctx_count
    skip = jnp.broadcast_to(channel_skip_scale[:, None], (block, 128))
    summed = convolve(group_long_filters, skip, mixture, rows_with(norms, tokens))
    sent = after(summed, far_part, got)
    received = lax.all_to_all(sent, "ctx", split_axis=0, concat_axis=0, tiled=True)
    part = after(parts[1], sent)
    other_part = exchange(part, "ctx", coarse)
    got = finish(part, [0], rest, cuts[1], cuts[2] - cuts[1])
    gating = gate(after(query, received, got, other_part), received)
    far_gating = exchange(gating, "ctx", half)
    owned = half * rows // 2
    norms_here = norms_of(after(received, gating), block, rows)
    norms_here = lax.dynamic_slice_in_dim(norms_here, tp_index * owned, owned)
    magnitude_here = lax.dynamic_slice_in_dim(magnitude, tp_index * owned, owned)
    scaling = magnitude_here / jnp.sqrt(norms_here + EPSILON)

    finish(after(far_part, received), [coarse], rest, 0, cuts[1])
    finish(after(other_part, received), [coarse], rest, cuts[1], cuts[2] - cuts[1])
    part = parts[2]
    late_start, late_rows = cuts[2], cuts[3] - cuts[2]
    if len(rest) == 1:
        upper = late_rows // 2 // 16 * 16
        coarse_part = exchange(after(part, scaling), "ctx", coarse)
        fine_part = exchange(after(part, received), "ctx", rest[0])
        last = exchange(coarse_part[:upper], "ctx", rest[0])
        other = exchange(fine_part[upper:], "ctx", coarse)
        pieces += [part, coarse_part, fine_part, last, other]
        layout += [((late_start, late_rows, index),) for index in (0, coarse, rest[0])]
        layout.append(((late_start, upper, coarse + rest[0]),))
        layout.append(((late_start + upper, late_rows - upper, coarse + rest[0]),))
    else:
        finish(after(part, scaling), [0], distances, late_start, late_rows)
    layout = tuple(layout)

    def place(h, l, y, c):
        return (h * half + l) * tp_count + y * 2 + c

    sites = [(h, l, c) for h in range(2) for l in range(half) for c in range(2)]

    def send_on(value, route):
        pairs = [route(h, l, c) for h, l, c in sites]
        return lax.ppermute(value, ("ctx", "tp"), [(place(*a), place(*b)) for a, b in pairs])

    near, far, sent = project(where, half, layout, pieces, gating, far_gating)
    received = exchange(sent, "tp", 1).astype(F32)
    far = far + received[1]
    split = owned // 2
    mine = lax.dynamic_slice_in_dim(far, upper_tp * split, split)
    theirs = lax.dynamic_slice_in_dim(far, (1 - upper_tp) * split, split).astype(BF16)
    far = (mine + exchange(theirs, "tp", 2).astype(F32)).astype(BF16)
    straight = send_on(far, lambda h, l, c: ((h, l, h, c), (1 - h, l, h, c)))
    diagonal = send_on(far, lambda h, l, c: ((h, l, 1 - h, c), (1 - h, l, h, c)))
    near = (near + received[0]).astype(BF16)
    from_near = send_on(near, lambda h, l, c: ((h, l, 1 - h, c), (h, l, h, c)))
    from_far = jnp.where(
        upper_tp == 0,
        jnp.concatenate([straight, diagonal], axis=0),
        jnp.concatenate([diagonal, straight], axis=0),
    )
    near = near.astype(F32) + from_near.astype(F32)
    out = jnp.where(upper_tp == high, near, from_far.astype(F32))
    return (out * scaling[:, None]).astype(BF16)


def solution(mesh):
    placed = (
        P(None, "tp", "ctx"),
        P(None, None, "tp"),
        P(("tp", "ctx")),
        P(("tp", "ctx"), None),
        P("ctx", "tp"),
        P(None, "tp"),
        P("ctx", None),
        P(),
    )
    return jax.shard_map(
        on_device, mesh=mesh, in_specs=placed, out_specs=P("tp", "ctx"), check_vma=False
    )
```

```python
import functools
import math

import jax
import jax.numpy as jnp
from jax import lax
from jax.experimental import pallas as pl
from jax.experimental.pallas import tpu as pltpu
from jax.sharding import PartitionSpec as P

GROUP = 16
TAPS = 7
EPSILON = 1e-06
MIB = 1 << 20
VMEM_LIMIT = 24 * MIB
PROJECT_LIMIT = 56 * MIB
BF16 = jnp.bfloat16
F32 = jnp.float32


def exchange(block, axis, distance):
    count = lax.axis_size(axis)
    return lax.ppermute(block, axis, [(i, i ^ distance) for i in range(count)])


def whole_spec(shape):
    return pl.BlockSpec(shape, lambda *_: (0,) * len(shape))


def tail_kernel(input_ref, out_ref):
    rows = []
    for i in range(3):
        turned = input_ref[i].astype(F32).T
        rows.append(turned[turned.shape[0] - 8 :])
    rows.append(jnp.zeros_like(rows[0]))
    out_ref[...] = jnp.concatenate(rows, axis=0).astype(BF16)


def last_tokens(values):
    width, tokens = values.shape[1:]
    lanes = min(width, 512)
    return pl.pallas_call(
        tail_kernel,
        grid=(width // lanes,),
        in_specs=[pl.BlockSpec((3, lanes, 128), lambda c: (0, c, tokens // 128 - 1))],
        out_specs=pl.BlockSpec((32, lanes), lambda c: (0, c)),
        out_shape=jax.ShapeDtypeStruct((32, width), BF16),
        compiler_params=pltpu.CompilerParams(vmem_limit_bytes=VMEM_LIMIT),
        name="last_tokens",
    )(values)


def merge_kernel(cuts, frozen_ref, down_ref, up_ref, *refs):
    norms_ref, part_refs = refs[-1], refs[-1 - len(cuts) + 1 : -1]
    for part_ref, start, end in zip(part_refs, cuts, cuts[1:]):
        update = jnp.dot(up_ref[start:end, :], down_ref[...], preferred_element_type=F32)
        merged = (frozen_ref[start:end, :].astype(F32) + update).astype(BF16)
        part_ref[...] = merged
        squares = jnp.square(merged.astype(F32))
        norms_ref[start:end, :] = jnp.broadcast_to(
            jnp.sum(squares, axis=1, keepdims=True), (end - start, 128)
        )


def merge(cuts, frozen, down, up, *others):
    rows, width = frozen.shape
    return pl.pallas_call(
        functools.partial(merge_kernel, cuts),
        in_specs=[pl.BlockSpec(memory_space=pltpu.VMEM)] * 3
        + [pl.BlockSpec(memory_space=pl.ANY)] * len(others),
        out_shape=[
            jax.ShapeDtypeStruct((end - start, width), BF16) for start, end in zip(cuts, cuts[1:])
        ]
        + [jax.ShapeDtypeStruct((rows, 128), F32)],
        compiler_params=pltpu.CompilerParams(vmem_limit_bytes=VMEM_LIMIT),
        name="merge",
    )(frozen, down, up, *others)


def featurize_kernel(input_ref, taps_ref, halo_ref, mixture_ref, query_ref, held):
    block, tokens = mixture_ref.shape[1:]

    @pl.loop(0, input_ref.shape[1] // 128, unroll=math.gcd(4, input_ref.shape[1] // 128))
    def _(tile):
        channels = pl.ds(pl.multiple_of(tile * 128, 128), 128)
        weights = []
        for i in range(3):
            weights.append(taps_ref[i, :, channels])
            held[i, :8, :] = halo_ref[:, channels].astype(F32)[8 * i : 8 * i + 8]
            held[i, 8:, :] = input_ref[i, channels, :].T.astype(F32)
        for place in range(0, tokens, 128):
            sums = []
            for i in range(3):
                total = weights[i][0:1, :] * held[i, 8 + place : 136 + place, :]
                for j in range(1, TAPS):
                    total += weights[i][j : j + 1, :] * held[i, 8 + place - j : 136 + place - j, :]
                sums.append(total)
            columns = slice(place, place + 128)
            mixture = (sums[1] * sums[2]).astype(BF16).T
            query = sums[0].astype(BF16).T
            if block >= 128:
                rows = pl.ds(pl.multiple_of(lax.rem(tile * 128, block), 128), 128)
                mixture_ref[tile * 128 // block, rows, columns] = mixture
                query_ref[tile * 128 // block, rows, columns] = query
            else:
                for n in range(128 // block):
                    rows = slice(n * block, (n + 1) * block)
                    mixture_ref[tile * (128 // block) + n, :, columns] = mixture[rows]
                    query_ref[tile * (128 // block) + n, :, columns] = query[rows]


def featurize(values, taps, halo, ctx_count):
    width, tokens = values.shape[1:]
    shape = jax.ShapeDtypeStruct((ctx_count, width // ctx_count, tokens), BF16)
    return pl.pallas_call(
        featurize_kernel,
        in_specs=[pl.BlockSpec(memory_space=pltpu.VMEM)] * 3,
        out_specs=[pl.BlockSpec(memory_space=pltpu.VMEM)] * 2,
        out_shape=[shape] * 2,
        scratch_shapes=[pltpu.VMEM((3, 8 + tokens, 128), F32)],
        compiler_params=pltpu.CompilerParams(vmem_limit_bytes=VMEM_LIMIT),
        cost_estimate=pl.CostEstimate(
            flops=6 * TAPS * width * tokens, bytes_accessed=10 * MIB, transcendentals=0
        ),
        name="featurize",
    )(values, taps, halo)


def convolve_kernel(filters_ref, skip_ref, mixture_ref, added_ref, result_ref, total_ref, out_ref, sems):
    ctx_count, block, tokens = mixture_ref.shape
    rows = ctx_count * GROUP

    def copy_out(group):
        place = (slice(None), pl.ds(pl.multiple_of(group * GROUP, GROUP), GROUP))
        return pltpu.make_async_copy(out_ref.at[place], result_ref.at[place], sems.at[group])

    for j in range(ctx_count):
        out_ref[j, block:, :] = added_ref[...]
    copy_out(block // GROUP).start()
    upper = lax.broadcasted_iota(jnp.int32, (tokens, tokens), 1) >= lax.broadcasted_iota(
        jnp.int32, (tokens, tokens), 0
    )

    @pl.loop(0, filters_ref.shape[0], unroll=math.gcd(4, filters_ref.shape[0]))
    def _(group):
        channels = pl.ds(pl.multiple_of(group * GROUP, GROUP), GROUP)
        here = pl.ds(group, 1)
        mixture = mixture_ref[:, channels, :]
        left = mixture.reshape(rows, tokens)

        def turned(start):
            taps = jnp.broadcast_to(filters_ref[here, pl.ds(start, tokens)], (tokens, tokens))
            return pltpu.roll(taps, 0, 1, stride=1, stride_axis=0)

        def product(count, these, before):
            matrix = jnp.where(upper, these, before).astype(BF16)
            return jnp.dot(left[:count], matrix, preferred_element_type=F32)

        before = turned(0)
        total_ref[:rows, :] = product(rows, before, 0.0)
        if ctx_count <= 8:
            for d in range(1, ctx_count):
                these = turned(d * tokens)
                total_ref[d * GROUP :, :] += product(rows - d * GROUP, these, before)
                before = these
        else:

            @pl.loop(1, ctx_count)
            def _(d):
                start = pl.multiple_of(d * tokens, tokens)
                place = pl.ds(pl.multiple_of(d * GROUP, GROUP), rows)
                matrices = turned(start), turned(start - tokens)
                total_ref[place, :] = total_ref[place, :] + product(rows, *matrices)

        skip = jnp.concatenate([skip_ref[channels, :]] * (tokens // 128), axis=1)
        for j in range(ctx_count):
            total = total_ref[j * GROUP : (j + 1) * GROUP, :]
            out_ref[j, channels, :] = (total + skip * mixture[j].astype(F32)).astype(BF16)
        copy_out(group).start()

    @pl.loop(0, block // GROUP + 1)
    def _(group):
        copy_out(group).wait()


def convolve(filters, skip, mixture, added):
    ctx_count, block, tokens = mixture.shape
    total_rows = ctx_count * GROUP * (1 if ctx_count <= 8 else 2)
    return pl.pallas_call(
        convolve_kernel,
        in_specs=[pl.BlockSpec(memory_space=pltpu.VMEM)] * 4,
        out_specs=pl.BlockSpec(memory_space=pl.ANY),
        scratch_shapes=[
            pltpu.VMEM((total_rows, tokens), F32),
            pltpu.VMEM((ctx_count, block + GROUP, tokens), BF16),
            pltpu.SemaphoreType.DMA((block // GROUP + 1,)),
        ],
        out_shape=jax.ShapeDtypeStruct((ctx_count, block + GROUP, tokens), BF16),
        compiler_params=pltpu.CompilerParams(vmem_limit_bytes=VMEM_LIMIT),
        cost_estimate=pl.CostEstimate(
            flops=8 * block * (ctx_count * tokens) ** 2, bytes_accessed=20 * MIB, transcendentals=0
        ),
        name="convolve",
    )(filters, skip, mixture, added)


def gate_kernel(query_ref, summed_ref, out_ref):
    ctx_count, block = query_ref.shape[:2]
    for d in range(ctx_count):
        product = query_ref[d].astype(F32) * summed_ref[d, :block, :].astype(F32)
        out_ref[d * block : (d + 1) * block, :] = product.astype(BF16)


def gate(query, summed):
    ctx_count, block, tokens = query.shape
    return pl.pallas_call(
        gate_kernel,
        in_specs=[pl.BlockSpec(memory_space=pltpu.VMEM)] * 2,
        out_specs=pl.BlockSpec(memory_space=pltpu.VMEM),
        out_shape=jax.ShapeDtypeStruct((ctx_count * block, tokens), BF16),
        compiler_params=pltpu.CompilerParams(vmem_limit_bytes=VMEM_LIMIT),
        name="gate",
    )(query, summed)


def project_kernel(layout, places, where_ref, gating_ref, far_gating_ref, *refs):
    arrays = len(layout)
    weight_refs = refs[:arrays]
    keep_refs, far_keep_refs, send_ref = refs[arrays : arrays + 3]
    held, gating_held, kept, sent, sems, out_sems = refs[arrays + 3 :]
    low, core = where_ref[1], where_ref[2]
    tokens = gating_ref.shape[1]
    block = 2 * keep_refs.shape[0] // places
    copies, at = [], 0
    for n, source in enumerate((gating_ref, far_gating_ref)):
        target = gating_held.at[:, pl.ds(n * tokens, tokens)]
        copies.append(pltpu.make_async_copy(source, target, sems.at[n]))
    for n, weight_ref in enumerate(weight_refs):
        rows = weight_ref.shape[0]
        target = held.at[pl.ds(at, rows), :]
        copies.append(pltpu.make_async_copy(weight_ref, target, sems.at[n + 2]))
        at += rows
    for copy in copies:
        copy.start()
    copies[0].wait()
    copies[1].wait()
    pending, outs, first, at = [], [], 0, 0
    total_rows = held.shape[0]
    for n, (copy, entries) in enumerate(zip(copies[2:], layout)):
        copy.wait()
        for entry in entries:
            pending.append((at, entry))
            at += entry[1]
        if at - first < (total_rows // 4 if first else total_rows // 8) and n + 1 < arrays:
            continue
        total = jnp.dot(held[first:at, :], gating_held[...], preferred_element_type=F32)
        for begin, (offset, rows, p) in pending:
            place = jnp.bitwise_xor(low, p)
            mine = place // (places // 2) == core
            start = (place & (places // 2 - 1)) * block + offset
            target = pl.ds(pl.multiple_of(start, 16), rows)
            piece = total[begin - first : begin - first + rows]
            here = slice(begin, begin + rows)
            sem = [out_sems.at[len(outs), n] for n in range(2)]
            keeping = [
                pltpu.make_async_copy(kept.at[0, here, :], keep_refs.at[target, :], sem[0]),
                pltpu.make_async_copy(kept.at[1, here, :], far_keep_refs.at[target, :], sem[1]),
            ]
            sending = [
                pltpu.make_async_copy(sent.at[n, here, :], send_ref.at[n, target, :], sem[n])
                for n in range(2)
            ]
            outs.append((mine, keeping, sending))

            @pl.when(mine)
            def _():
                for n in range(2):
                    kept[n, here, :] = piece[:, n * tokens : (n + 1) * tokens]
                    keeping[n].start()

            @pl.when(jnp.logical_not(mine))
            def _():
                for n in range(2):
                    sent[n, here, :] = piece[:, n * tokens : (n + 1) * tokens].astype(BF16)
                    sending[n].start()

        pending, first = [], at
    for mine, keeping, sending in outs:

        @pl.when(mine)
        def _():
            for copy in keeping:
                copy.wait()

        @pl.when(jnp.logical_not(mine))
        def _():
            for copy in sending:
                copy.wait()


def project(where, places, layout, weights, gating, far_gating):
    width, tokens = gating.shape
    total_rows = sum(weight.shape[0] for weight in weights)
    out = jax.ShapeDtypeStruct((total_rows // 2, tokens), F32)
    sent = jax.ShapeDtypeStruct((2, total_rows // 2, tokens), BF16)
    return pl.pallas_call(
        functools.partial(project_kernel, layout, places),
        grid_spec=pltpu.PrefetchScalarGridSpec(
            num_scalar_prefetch=1,
            grid=(1,),
            in_specs=[pl.BlockSpec(memory_space=pl.ANY)] * (2 + len(weights)),
            out_specs=[pl.BlockSpec(memory_space=pl.ANY)] * 3,
            scratch_shapes=[
                pltpu.VMEM((total_rows, width), BF16),
                pltpu.VMEM((width, 2 * tokens), BF16),
                pltpu.VMEM((2, total_rows, tokens), F32),
                pltpu.VMEM((2, total_rows, tokens), BF16),
                pltpu.SemaphoreType.DMA((len(weights) + 2,)),
                pltpu.SemaphoreType.DMA((sum(map(len, layout)), 2)),
            ],
        ),
        out_shape=[out, out, sent],
        compiler_params=pltpu.CompilerParams(vmem_limit_bytes=PROJECT_LIMIT),
        cost_estimate=pl.CostEstimate(
            flops=4 * total_rows * tokens * width, bytes_accessed=10 * MIB, transcendentals=0
        ),
        name="project",
    )(where, gating, far_gating, *weights)


def after(value, *others):
    return lax.optimization_barrier((value, *others))[0]


def rows_with(norms, tokens):
    flat = norms.reshape(-1)
    flat = jnp.pad(flat, (0, -flat.shape[0] % tokens)).reshape(-1, tokens)
    pieces = []
    for _ in range(3):
        piece = lax.optimization_barrier(flat.astype(BF16))
        pieces.append(piece)
        flat = flat - piece.astype(F32)
    added = jnp.concatenate(pieces)
    return jnp.pad(added, ((0, GROUP - added.shape[0]), (0, 0)))


def norms_of(received, block, rows):
    ctx_count, _, tokens = received.shape
    lines = -(-rows // tokens)
    added = received[:, block : block + 3 * lines].astype(F32)
    added = added.reshape(ctx_count, 3, lines * tokens)
    return (added[:, 0] + (added[:, 1] + added[:, 2]))[:, :rows].reshape(ctx_count * rows)


def on_device(
    query_key_value_input,
    featurizer_weights,
    channel_skip_scale,
    group_long_filters,
    frozen_weight,
    down_update_weight,
    up_update_weight,
    magnitude,
):
    width, tokens = query_key_value_input.shape[1:]
    ctx_count = lax.axis_size("ctx")
    tp_count = lax.axis_size("tp")
    half = ctx_count // 2
    rows = frozen_weight.shape[0]
    me = lax.axis_index("ctx")
    tp_index = lax.axis_index("tp")
    low = jnp.bitwise_and(me, half - 1)
    high = me // half
    core = jnp.bitwise_and(tp_index, 1)
    upper_tp = tp_index // 2
    where = jnp.stack([me, low, core, high]).astype(jnp.int32)

    tail = last_tokens(query_key_value_input)
    halo = lax.ppermute(tail, "ctx", [(i, i + 1) for i in range(ctx_count - 1)])

    mixture, query = featurize(query_key_value_input, featurizer_weights, halo, ctx_count)
    own_mixture = mixture
    mixture = lax.all_to_all(own_mixture, "ctx", split_axis=0, concat_axis=0, tiled=True)

    cuts = (0, rows * 12 // 32 // 16 * 16, rows * 21 // 32 // 16 * 16, rows)
    frozen = after(frozen_weight, own_mixture)
    *parts, norms = merge(cuts, frozen, down_update_weight, up_update_weight)
    norms = norms[:, 0][None, :]
    norms = norms + sum(exchange(norms, "tp", distance) for distance in range(1, tp_count))

    distances = []
    while 1 << len(distances) < half:
        distances.insert(0, 1 << len(distances))
    coarse, rest = distances[0], distances[1:]
    pieces, layout = [], []

    def finish(held, order, path, offset, length):
        for distance in path[:-1]:
            received = exchange(held, "ctx", distance)
            held = jnp.concatenate([held, received], axis=0)
            order = order + [index + distance for index in order]
        received = exchange(held, "ctx", path[-1])
        pieces.extend([held, received])
        layout.append(tuple((offset, length, index) for index in order))
        layout.append(tuple((offset, length, index + path[-1]) for index in order))
        return received

    part = parts[0]
    far_part = exchange(part, "ctx", coarse)
    got = finish(part, [0], rest, 0, cuts[1])
    block = width // ctx_count
    skip = jnp.broadcast_to(channel_skip_scale[:, None], (block, 128))
    summed = convolve(group_long_filters, skip, mixture, rows_with(norms, tokens))
    sent = after(summed, far_part, got)
    received = lax.all_to_all(sent, "ctx", split_axis=0, concat_axis=0, tiled=True)
    part = after(parts[1], sent)
    other_part = exchange(part, "ctx", coarse)
    got = finish(part, [0], rest, cuts[1], cuts[2] - cuts[1])
    gating = gate(after(query, received, got), received)
    far_gating = exchange(gating, "ctx", half)
    owned = half * rows // 2
    norms_here = norms_of(after(received, gating), block, rows)
    norms_here = lax.dynamic_slice_in_dim(norms_here, tp_index * owned, owned)
    magnitude_here = lax.dynamic_slice_in_dim(magnitude, tp_index * owned, owned)
    scaling = magnitude_here / jnp.sqrt(norms_here + EPSILON)

    finish(after(far_part, received), [coarse], rest, 0, cuts[1])
    finish(after(other_part, received), [coarse], rest, cuts[1], cuts[2] - cuts[1])
    part = parts[2]
    late_start, late_rows = cuts[2], cuts[3] - cuts[2]
    if len(rest) == 1:
        upper = late_rows // 2 // 16 * 16
        coarse_part = exchange(after(part, scaling), "ctx", coarse)
        fine_part = exchange(after(part, received), "ctx", rest[0])
        last = exchange(coarse_part[:upper], "ctx", rest[0])
        other = exchange(fine_part[upper:], "ctx", coarse)
        pieces += [part, coarse_part, fine_part, last, other]
        layout += [((late_start, late_rows, index),) for index in (0, coarse, rest[0])]
        layout.append(((late_start, upper, coarse + rest[0]),))
        layout.append(((late_start + upper, late_rows - upper, coarse + rest[0]),))
    else:
        finish(after(part, scaling), [0], distances, late_start, late_rows)
    layout = tuple(layout)

    def place(h, l, y, c):
        return (h * half + l) * tp_count + y * 2 + c

    sites = [(h, l, c) for h in range(2) for l in range(half) for c in range(2)]

    def send_on(value, route):
        pairs = [route(h, l, c) for h, l, c in sites]
        return lax.ppermute(value, ("ctx", "tp"), [(place(*a), place(*b)) for a, b in pairs])

    near, far, sent = project(where, half, layout, pieces, gating, far_gating)
    received = exchange(sent, "tp", 1).astype(F32)
    far = far + received[1]
    split = owned // 2
    mine = lax.dynamic_slice_in_dim(far, upper_tp * split, split)
    theirs = lax.dynamic_slice_in_dim(far, (1 - upper_tp) * split, split).astype(BF16)
    far = (mine + exchange(theirs, "tp", 2).astype(F32)).astype(BF16)
    straight = send_on(far, lambda h, l, c: ((h, l, h, c), (1 - h, l, h, c)))
    diagonal = send_on(far, lambda h, l, c: ((h, l, 1 - h, c), (1 - h, l, h, c)))
    near = (near + received[0]).astype(BF16)
    from_near = send_on(near, lambda h, l, c: ((h, l, 1 - h, c), (h, l, h, c)))
    from_far = jnp.where(
        upper_tp == 0,
        jnp.concatenate([straight, diagonal], axis=0),
        jnp.concatenate([diagonal, straight], axis=0),
    )
    near = near.astype(F32) + from_near.astype(F32)
    out = jnp.where(upper_tp == high, near, from_far.astype(F32))
    return (out * scaling[:, None]).astype(BF16)


def solution(mesh):
    placed = (
        P(None, "tp", "ctx"),
        P(None, None, "tp"),
        P(("tp", "ctx")),
        P(("tp", "ctx"), None),
        P("ctx", "tp"),
        P(None, "tp"),
        P("ctx", None),
        P(),
    )
    return jax.shard_map(
        on_device, mesh=mesh, in_specs=placed, out_specs=P("tp", "ctx"), check_vma=False
    )
```
